32 devices in a mesh: dp: 8 (over z, x), mp: 4 (over y, core).
Axes of the slice: x: 2, y: 2, z: 4, core: 2. Of those that a mesh axis runs over, the one named last changes fastest.
Arguments:
- activations: bfloat16 [20480, 1024], P(('dp', 'mp')), may hold values from -6 to 6
- cotangent: bfloat16 [20480, 1024], P('dp'), may hold values from -6 to 6
- layout: int32 [32], P('dp'), may hold values from 0 to 2
- band_ids: int32 [32], P('dp'), may hold values from 0 to 7
- condition: float32 [8, 1024], replicated, may hold values from -6 to 6
- qkv_weight: float32 [1024, 3072], P('dp', 'mp'), may hold values from -0.1875 to 0.1875
- qkv_moment: float32 [1024, 3072], P('dp', 'mp'), may hold values from -40 to 40
- qkv_square: float32 [1024, 3072], P('dp', 'mp'), may hold values from 2.048 to 20.48
- out_weight: float32 [1024, 1024], P('dp', 'mp'), may hold values from -0.75 to 0.75
- out_moment: float32 [1024, 1024], P('dp', 'mp'), may hold values from -40 to 40
- out_square: float32 [1024, 1024], P('dp', 'mp'), may hold values from 2.048 to 20.48
- up_weight: float32 [1024, 4096], P('dp', 'mp'), may hold values from -0.1875 to 0.1875
- up_moment: float32 [1024, 4096], P('dp', 'mp'), may hold values from -40 to 40
- up_square: float32 [1024, 4096], P('dp', 'mp'), may hold values from 2.048 to 20.48
- down_weight: float32 [1024, 4096], P('dp', 'mp'), may hold values from -0.09375 to 0.09375
- down_moment: float32 [1024, 4096], P('dp', 'mp'), may hold values from -40 to 40
- down_square: float32 [1024, 4096], P('dp', 'mp'), may hold values from 2.048 to 20.48
- ada_weight: float32 [1024, 6144], P('dp'), may hold values from -0.375 to 0.375
- ada_moment: float32 [1024, 6144], P('dp'), may hold values from -40 to 40
- ada_square: float32 [1024, 6144], P('dp'), may hold values from 2.048 to 20.48
- bias_table: float32 [16, 45], P('mp'), may hold values from -4 to 4
- bias_moment: float32 [16, 45], P('mp'), may hold values from -40 to 40
- bias_square: float32 [16, 45], P('mp'), may hold values from 2.048 to 20.48
Outputs:
- layer_out: bfloat16 [20480, 1024], P(('dp', 'mp'))
- input_grad: float32 [20480, 1024], P(('dp', 'mp'))
- qkv_new: float32 [1024, 3072], P('dp', 'mp')
- qkv_moment_new: float32 [1024, 3072], P('dp', 'mp')
- qkv_square_new: float32 [1024, 3072], P('dp', 'mp')
- out_new: float32 [1024, 1024], P('dp', 'mp')
- out_moment_new: float32 [1024, 1024], P('dp', 'mp')
- out_square_new: float32 [1024, 1024], P('dp', 'mp')
- up_new: float32 [1024, 4096], P('dp', 'mp')
- up_moment_new: float32 [1024, 4096], P('dp', 'mp')
- up_square_new: float32 [1024, 4096], P('dp', 'mp')
- down_new: float32 [1024, 4096], P('dp', 'mp')
- down_moment_new: float32 [1024, 4096], P('dp', 'mp')
- down_square_new: float32 [1024, 4096], P('dp', 'mp')
- ada_new: float32 [1024, 6144], P('dp')
- ada_moment_new: float32 [1024, 6144], P('dp')
- ada_square_new: float32 [1024, 6144], P('dp')
- bias_new: float32 [16, 45], P('mp')
- bias_moment_new: float32 [16, 45], P('mp')
- bias_square_new: float32 [16, 45], P('mp')
- lamb_stats: float32 [3, 6], replicated
The draws below stay inside these ranges and needn't reach their ends.
Inputs may be any that keep to these rules, and one draw needn't show every extreme that they name: `layout`: 0: two windows of 5 x 8 x 8 tokens; 1: one such window, then five single-frame 8 x 8 windows; 2: ten single-frame 8 x 8 windows.
All inputs are finite; a program needn't handle non-finite values.
Results may differ from the reference program's by a relative error of at most 0.02.
The reference program's roundings to bfloat16 on the way count: a program that leaves them out, or rounds other values in their place, can miss the bound.
Values may be sent and summed in bfloat16 or wider, within the bound.
No kernel may reach another device: no remote copies, remote signals or barrier semaphores. Data moves between devices by JAX's collectives and lax.ppermute only.
A program may use at most 192 MiB of HBM per device.

```python
import math
import jax
import jax.numpy as jnp
import numpy as np
from jax import lax

D = 1024
H = 16
FF = 4096
BLOCK = 640
BANDS = 8
STEP = 10
TOKENS = 20480
BLOCKS = 32


def touch_ends(array, rng, low, top_value):
    dims = array.shape
    spot = [jax.random.randint(jax.random.fold_in(rng, axis), (), 0, dims[axis]) for axis in range(len(dims))]
    array = array.at[tuple(spot)].set(low)
    longest = dims.index(max(dims))
    spot[longest] = (spot[longest] + 1) % dims[longest]
    return array.at[tuple(spot)].set(top_value)


def block_levels(stream_key, extent, shards, smallest, largest):
    factor_of, own = 1.0, jax.random.fold_in(stream_key, 6)
    for axis_at, blocks in shards:
        steps = jnp.exp(jax.random.uniform(jax.random.fold_in(own, axis_at), (blocks,), jnp.float32, smallest / len(shards), largest / len(shards)))
        factor_of = factor_of * jnp.repeat(steps, extent[axis_at] // blocks).reshape([-1 if axis == axis_at else 1 for axis in range(len(extent))])
    return factor_of


def cumulative_ranks(count, slope):
    loads = [(1 << 20) // math.isqrt(grade ** slope) + 1 for grade in range(1, count + 1)]
    width = 1 + sum(loads) // (1 << 30)
    return np.cumsum(np.array([max(1, weight // width) for weight in loads]))


def skewed_ids(stream_key, extent, number_of, lean):
    listing = cumulative_ranks(number_of, lean)
    lot = jax.random.randint(jax.random.fold_in(stream_key, 1), extent, 0, int(listing[number_of - 1]))
    standing = jnp.searchsorted(jnp.asarray(listing, jnp.int32), lot, side="right")
    return jax.random.permutation(jax.random.fold_in(stream_key, 2), number_of)[standing].astype(jnp.int32)


def bell_draw(own_key, extent, scale, bound, cuts=(), held_as=jnp.bfloat16):
    gain = block_levels(own_key, extent, cuts, -0.22, 0.18) if cuts else 1.0
    drawn = jax.random.normal(own_key, extent, jnp.float32) * scale * gain
    return jnp.minimum(jnp.maximum(drawn, -bound), bound).astype(held_as)


def setup_inputs(seed: int = 0) -> dict:
    splits = jax.random.split(jax.random.key(seed), 24)
    return {
        "activations": bell_draw(splits[0], (TOKENS, D), 1.0, 6.0, ((0, 32),)),
        "cotangent": bell_draw(splits[1], (TOKENS, D), 1.0, 6.0, ((0, 8),)),
        "layout": touch_ends(jax.random.randint(splits[2], (BLOCKS,), 0, 3), jax.random.fold_in(splits[2], 1), 0, 2).astype(jnp.int32),
        "band_ids": touch_ends(skewed_ids(splits[3], (BLOCKS,), BANDS, 2), jax.random.fold_in(splits[3], 3), 0, BANDS - 1).astype(jnp.int32),
        "condition": bell_draw(splits[4], (BANDS, D), 1.0, 6.0, (), jnp.float32),
        "qkv_weight": bell_draw(splits[5], (D, 3 * D), D ** -0.5, 0.1875, ((0, 8), (1, 4)), jnp.float32),
        "qkv_moment": bell_draw(splits[6], (D, 3 * D), (TOKENS ** 0.5 * 0.05), 40.0, ((0, 8), (1, 4)), jnp.float32),
        "qkv_square": jnp.clip(jnp.exp(math.log(20.48) - 2.30258502 * jax.random.uniform(splits[7], (D, 3 * D), jnp.float32) ** block_levels(splits[7], (D, 3 * D), ((0, 8), (1, 4)), -0.2, 0.2)), 2.048, 20.48),
        "out_weight": bell_draw(splits[8], (D, D), (D // 16) ** -0.5, 0.75, ((0, 8), (1, 4)), jnp.float32),
        "out_moment": bell_draw(splits[9], (D, D), (TOKENS ** 0.5 * 0.05), 40.0, ((0, 8), (1, 4)), jnp.float32),
        "out_square": jnp.clip(jnp.exp(math.log(20.48) - 2.30258502 * jax.random.uniform(splits[10], (D, D), jnp.float32) ** block_levels(splits[10], (D, D), ((0, 8), (1, 4)), -0.2, 0.2)), 2.048, 20.48),
        "up_weight": bell_draw(splits[11], (D, FF), D ** -0.5, 0.1875, ((0, 8), (1, 4)), jnp.float32),
        "up_moment": bell_draw(splits[12], (D, FF), (TOKENS ** 0.5 * 0.05), 40.0, ((0, 8), (1, 4)), jnp.float32),
        "up_square": jnp.clip(jnp.exp(math.log(20.48) - 2.30258502 * jax.random.uniform(splits[13], (D, FF), jnp.float32) ** block_levels(splits[13], (D, FF), ((0, 8), (1, 4)), -0.2, 0.2)), 2.048, 20.48),
        "down_weight": bell_draw(splits[14], (D, FF), FF ** -0.5, 0.09375, ((0, 8), (1, 4)), jnp.float32),
        "down_moment": bell_draw(splits[15], (D, FF), (TOKENS ** 0.5 * 0.05), 40.0, ((0, 8), (1, 4)), jnp.float32),
        "down_square": jnp.clip(jnp.exp(math.log(20.48) - 2.30258502 * jax.random.uniform(splits[16], (D, FF), jnp.float32) ** block_levels(splits[16], (D, FF), ((0, 8), (1, 4)), -0.2, 0.2)), 2.048, 20.48),
        "ada_weight": bell_draw(splits[17], (D, 6 * D), (D // 4) ** -0.5, 0.375, ((0, 8),), jnp.float32),
        "ada_moment": bell_draw(splits[18], (D, 6 * D), (TOKENS ** 0.5 * 0.05), 40.0, ((0, 8),), jnp.float32),
        "ada_square": jnp.clip(jnp.exp(math.log(20.48) - 2.30258502 * jax.random.uniform(splits[19], (D, 6 * D), jnp.float32) ** block_levels(splits[19], (D, 6 * D), ((0, 8),), -0.2, 0.2)), 2.048, 20.48),
        "bias_table": bell_draw(splits[20], (H, 45), 0.7, 4.0, ((0, 4),), jnp.float32),
        "bias_moment": bell_draw(splits[21], (H, 45), (TOKENS ** 0.5 * 0.05), 40.0, ((0, 4),), jnp.float32),
        "bias_square": jnp.clip(jnp.exp(math.log(20.48) - 2.30258502 * jax.random.uniform(splits[22], (H, 45), jnp.float32) ** block_levels(splits[22], (H, 45), ((0, 4),), -0.2, 0.2)), 2.048, 20.48),
    }


precise = lax.Precision.HIGHEST
beta_first = 0.9
beta_second = 0.999
adam_eps = 1e-06
weight_decay = 0.01
learn_rate = 0.3
norm_eps = 1e-06

@jax.custom_vjp
def low(v):
    return lax.optimization_barrier(v.astype(jnp.bfloat16)).astype(jnp.float32)

@jax.custom_vjp
def low_back(v):
    return v

def low_keep(v):
    return (low(v), None)

def low_pass(kept, grad):
    return (grad,)

def back_keep(v):
    return (v, None)

def back_low(kept, grad):
    return (low(grad),)
low.defvjp(low_keep, low_pass)
low_back.defvjp(back_keep, back_low)

def window_layout(layout):
    places = jnp.arange(BLOCK, dtype=jnp.int32)[None, :]
    large = (2 - layout)[:, None].astype(jnp.int32)
    border = large * (BLOCK // 2)
    inside = places < border
    window_ids = jnp.where(inside, places // (BLOCK // 2), large + (places - border) // (BLOCK // 10))
    frames = jnp.where(inside, places % (BLOCK // 2) // (BLOCK // 10), 0)
    rows_in = jnp.broadcast_to(places // 8 % 8, window_ids.shape)
    cols_in = jnp.broadcast_to(places % 8, window_ids.shape)
    return (window_ids, frames, rows_in, cols_in)

def normalize(values):
    centered = values - lax.optimization_barrier(jnp.mean(values, axis=-1, keepdims=True))
    return centered * lax.rsqrt(lax.optimization_barrier(jnp.mean(centered * centered, axis=-1, keepdims=True)) + norm_eps)

def block_layer(weights, inputs):
    qkv_low, out_low, up_low, down_low, table_full = weights
    rows_x, modul, window_ids, frames, rows_in, cols_in = inputs
    shift_one, scale_one, gate_one, shift_two, scale_two, gate_two = jnp.split(modul, 6)
    heads = table_full.shape[0]
    head_dim = rows_x.shape[1] // heads
    normed_one = low(normalize(rows_x) * (1.0 + scale_one) + shift_one)
    project = jnp.dot(normed_one, qkv_low, precision=precise)
    project = low_back(low(project)).reshape(BLOCK, heads, 3, head_dim)
    queries = project[:, :, 0]
    keys_blk = project[:, :, 1]
    values_blk = project[:, :, 2]
    scores = jnp.einsum('ihe,jhe->hij', queries, keys_blk, precision=precise) * head_dim ** (-0.5)
    offset_f = frames[:, None] - frames[None, :] + 7
    offset_r = rows_in[:, None] - rows_in[None, :] + 7
    offset_c = cols_in[:, None] - cols_in[None, :] + 7
    scores = scores + table_full[:, offset_f] + table_full[:, 15 + offset_r] + table_full[:, 30 + offset_c]
    scores = low_back(scores)
    same = window_ids[:, None] == window_ids[None, :]
    probs = low(jax.nn.softmax(jnp.where(same[None], scores, -1e+30), axis=-1))
    attended = jnp.einsum('hij,jhe->ihe', probs, values_blk, precision=precise).reshape(BLOCK, heads * head_dim)
    attended = low_back(low(attended))
    branch_one = low_back(jnp.dot(attended, out_low.T, precision=precise))
    middle = rows_x + gate_one * branch_one
    normed_two = low(normalize(middle) * (1.0 + scale_two) + shift_two)
    hidden_pre = low_back(jnp.dot(normed_two, up_low, precision=precise))
    hidden = low(jax.nn.gelu(hidden_pre, approximate=True))
    branch_two = low_back(jnp.dot(hidden, down_low.T, precision=precise))
    return middle + gate_two * branch_two

def lamb_update(weight, moment, square, gradient):
    moment_new = beta_first * moment + (1.0 - beta_first) * gradient
    square_new = beta_second * square + (1.0 - beta_second) * gradient * gradient
    direction = moment_new / (1.0 - beta_first ** STEP) / (jnp.sqrt(square_new / (1.0 - beta_second ** STEP)) + adam_eps) + weight_decay * weight
    weight_norm = jnp.sqrt(jnp.sum(weight * weight))
    update_norm = jnp.sqrt(jnp.sum(direction * direction))
    trust_ratio = weight_norm / update_norm
    return (weight - learn_rate * trust_ratio * direction, moment_new, square_new, weight_norm, update_norm, trust_ratio)

def reference(activations, cotangent, layout, band_ids, condition, qkv_weight, qkv_moment, qkv_square, out_weight, out_moment, out_square, up_weight, up_moment, up_square, down_weight, down_moment, down_square, ada_weight, ada_moment, ada_square, bias_table, bias_moment, bias_square):
    window_ids, frames, rows_in, cols_in = window_layout(layout)
    band_hot = (band_ids[:, None] == jnp.arange(BANDS, dtype=jnp.int32)[None, :]).astype(jnp.float32)
    cond_rows = jax.nn.silu(jnp.dot(band_hot, condition, precision=precise))
    rows_all = activations.astype(jnp.float32).reshape(BLOCKS, BLOCK, D)
    layer = jax.checkpoint(block_layer)

    def forward(qkv_w, out_w, up_w, down_w, ada_w, table_w, rows_x):
        cond_low = low(cond_rows)
        modul = low_back(jnp.dot(cond_low, low(ada_w), precision=precise))
        weights = (low(qkv_w), low(out_w), low(up_w), low(down_w), table_w)
        return lax.map(lambda inputs: layer(weights, inputs), (rows_x, modul, window_ids, frames, rows_in, cols_in))
    outputs, pullback = jax.vjp(forward, qkv_weight, out_weight, up_weight, down_weight, ada_weight, bias_table, rows_all)
    grads = pullback(cotangent.astype(jnp.float32).reshape(BLOCKS, BLOCK, D))
    qkv_new, qkv_m, qkv_s, qkv_wn, qkv_un, qkv_tr = lamb_update(qkv_weight, qkv_moment, qkv_square, grads[0])
    out_new, out_m, out_s, out_wn, out_un, out_tr = lamb_update(out_weight, out_moment, out_square, grads[1])
    up_new, up_m, up_s, up_wn, up_un, up_tr = lamb_update(up_weight, up_moment, up_square, grads[2])
    down_new, down_m, down_s, down_wn, down_un, down_tr = lamb_update(down_weight, down_moment, down_square, grads[3])
    ada_new, ada_m, ada_s, ada_wn, ada_un, ada_tr = lamb_update(ada_weight, ada_moment, ada_square, grads[4])
    bias_new, bias_m, bias_s, bias_wn, bias_un, bias_tr = lamb_update(bias_table, bias_moment, bias_square, grads[5])
    lamb_stats = jnp.stack([jnp.stack([qkv_wn, out_wn, up_wn, down_wn, ada_wn, bias_wn]), jnp.stack([qkv_un, out_un, up_un, down_un, ada_un, bias_un]), jnp.stack([qkv_tr, out_tr, up_tr, down_tr, ada_tr, bias_tr])])
    layer_out = outputs.reshape(TOKENS, D).astype(jnp.bfloat16)
    input_grad = grads[6].reshape(TOKENS, D)
    return (layer_out, input_grad, qkv_new, qkv_m, qkv_s, out_new, out_m, out_s, up_new, up_m, up_s, down_new, down_m, down_s, ada_new, ada_m, ada_s, bias_new, bias_m, bias_s, lamb_stats)
```

```python
from functools import partial

import jax
import jax.numpy as jnp
import numpy as np
from jax import lax
from jax.experimental import pallas as pl
from jax.experimental.pallas import tpu as pltpu
from jax.sharding import Mesh
from jax.sharding import PartitionSpec as P

BLOCK = 640
HALF = BLOCK // 2
FRAME = BLOCK // 10
LANES = 128
STEP = 10

precise = lax.Precision.HIGHEST
beta_first = 0.9
beta_second = 0.999
adam_eps = 1e-06
weight_decay = 0.01
learn_rate = 0.3
norm_eps = 1e-06
low = jnp.bfloat16
wide = jnp.float32
MIB = 1 << 20


def contract(left, right, left_dim, right_dim):
    return lax.dot_general(
        left, right, (((left_dim,), (right_dim,)), ((), ())), preferred_element_type=wide
    )


def lamb_direction(weight, moment, square, gradient):
    moment_new = beta_first * moment + (1.0 - beta_first) * gradient
    square_new = beta_second * square + (1.0 - beta_second) * gradient * gradient
    direction = (
        moment_new
        / (1.0 - beta_first**STEP)
        / (jnp.sqrt(square_new / (1.0 - beta_second**STEP)) + adam_eps)
        + weight_decay * weight
    )
    return (moment_new, square_new, direction)


def cut_sizes(count):
    sizes = []
    while count > 4:
        sizes.append(4)
        count //= 4
    sizes.append(count)
    return sizes


def from_xor(value, axes, mask):
    size = lax.axis_size(axes)
    return lax.ppermute(value, axes, [(at ^ mask, at) for at in range(size)])


def swap(value, axis):
    return from_xor(value, axis, 1)


def tree_sum(terms):
    while len(terms) > 1:
        terms = [terms[at] + terms[at + 1] for at in range(0, len(terms), 2)]
    return terms[0]


def sum_over(value, axes):
    size = lax.axis_size(axes)
    return tree_sum([value] + [from_xor(value, axes, mask) for mask in range(1, size)])


def in_pair(value, axis):
    other = swap(value, axis)
    first = lax.axis_index(axis) == 0
    return jnp.where(first, value, other), jnp.where(first, other, value)


def in_order(value, axis, dim):
    return jnp.concatenate(in_pair(value, axis), axis=dim)


def low_stages(low_axes):
    stages = []
    for axis in low_axes:
        size = lax.axis_size(axis)
        stages += [(axis, 3), (axis, 1)] if size == 4 else [(axis, 1)]
    return stages


def gather_low(shard, low_axes):
    stages = low_stages(low_axes)
    near = shard
    for axis, mask in stages[:-1]:
        near = jnp.concatenate([near, from_xor(near, axis, mask)], axis=0)
    return near, from_xor(near, *stages[-1])


def gather_rest(near, far, after):
    near_x = swap(near, "x")
    (near_x,) = gate((near_x,), after)
    near_both = jnp.concatenate([near, near_x], axis=0)
    far_other = swap(far, "y")
    near_other = swap(near_both, "y")
    far_x = swap(jnp.stack([far, far_other]), "x")
    return (near_both, far, near_other, far_other, far_x)


def gather_first(near, far):
    near_both = jnp.concatenate([near, swap(near, "x")], axis=0)
    (far,) = gate((far,), (near_both,))
    far_other = swap(far, "y")
    (near_both,) = gate((near_both,), (far_other,))
    near_other = swap(near_both, "y")
    stack = jnp.stack([far, far_other])
    return (near_both, far, near_other, far_other, swap(stack, "x")), stack


def chunk_order(low_axes):
    places = [{axis: lax.axis_index(axis) for axis in low_axes}]
    for axis, mask in low_stages(low_axes):
        places = places + [{**place, axis: place[axis] ^ mask} for place in places]
    order = []
    for place in places:
        base = jnp.int32(0)
        for axis in low_axes:
            base = base * lax.axis_size(axis) + place[axis]
        order.append(base)
    half = len(order) // 2
    x_here = lax.axis_index("x")
    full = []
    for part in (order[:half], order[half:]):
        for step in range(2):
            full = full + [base * 2 + (x_here ^ step) for base in part]
    return jnp.stack(full).astype(jnp.int32)


def sum_stages(value, low_axes):
    for axis, mask in low_stages(low_axes):
        value = value + from_xor(value, axis, mask)
    return value + swap(value, "x")


def is_large(shape):
    return np.prod(shape) >= 1 << 15


def stay(array):
    if is_large(array.shape):
        return pltpu.with_memory_space_constraint(array, pltpu.HBM)
    return array


FLOPS_PER_US = 1.15e9


def call(
    kernel,
    cost,
    grid,
    in_specs,
    out_specs,
    out_shapes,
    limit,
    args,
    scalars=(),
    deps=(),
    bases=(),
    stream=False,
):
    taken = len(scalars) + len(args)
    extra = (*bases, *deps)
    if stream:
        args = [stay(array) for array in args]

    def body(*refs):
        kernel(*refs[:taken], *refs[taken + len(extra) :])

    return pl.pallas_call(
        body,
        grid_spec=pltpu.PrefetchScalarGridSpec(
            num_scalar_prefetch=len(scalars),
            grid=grid,
            in_specs=[*in_specs, *[pl.BlockSpec(memory_space=pl.ANY)] * len(extra)],
            out_specs=out_specs,
        ),
        out_shape=[
            pltpu.HBM(shape, dtype)
            if stream and is_large(shape)
            else jax.ShapeDtypeStruct(shape, dtype)
            for shape, dtype in out_shapes
        ],
        input_output_aliases={taken + at: at for at in range(len(bases))},
        cost_estimate=pl.CostEstimate(
            flops=int(cost * FLOPS_PER_US), bytes_accessed=1, transcendentals=0
        ),
        compiler_params=pltpu.CompilerParams(vmem_limit_bytes=limit),
    )(*scalars, *args, *extra)


def gate_kernel(*_):
    pass


def gate(arrays, deps):
    return call(
        gate_kernel,
        0.5,
        (1,),
        [],
        [pl.BlockSpec(memory_space=pl.ANY)] * len(arrays),
        [(array.shape, array.dtype) for array in arrays],
        MIB,
        (),
        deps=deps,
        bases=arrays,
    )


def whole(array):
    zeros = (0,) * array.ndim
    return pl.BlockSpec(array.shape, lambda *_: zeros)


def take_chunks(values, order):
    rows, width = values.shape
    count = order.shape[0]
    return jnp.take(values.reshape(rows, count, width // count), order, axis=1).reshape(rows, width)


def inside(width, order):
    return width // order.shape[0] % LANES == 0


def load_chunks(ref, order_ref, moved):
    if not moved:
        return ref[...]
    count = order_ref.shape[0]
    chunk = ref.shape[1] // count
    return jnp.concatenate(
        [
            ref[:, pl.ds(pl.multiple_of(order_ref[at] * chunk, chunk), chunk)]
            for at in range(count)
        ],
        axis=1,
    )


def store_chunks(ref, order_ref, moved, values):
    if not moved:
        ref[...] = values
        return
    count = order_ref.shape[0]
    chunk = ref.shape[1] // count
    for at in range(count):
        ref[:, pl.ds(pl.multiple_of(order_ref[at] * chunk, chunk), chunk)] = values[
            :, at * chunk : (at + 1) * chunk
        ]


def normalize(values):
    centered = values - jnp.mean(values, axis=-1, keepdims=True)
    inverse = lax.rsqrt(jnp.mean(centered * centered, axis=-1, keepdims=True) + norm_eps)
    return centered * inverse, inverse


def norm_back(values, upstream, scale_row):
    normed, inverse = normalize(values)
    inner = upstream * (1.0 + scale_row)
    grad = (
        inner
        - jnp.mean(inner, axis=-1, keepdims=True)
        - normed * jnp.mean(inner * normed, axis=-1, keepdims=True)
    ) * inverse
    return normed, grad


def add_sums(ref, first, values):
    sums = jnp.concatenate([jnp.sum(value, axis=0, keepdims=True) for value in values], axis=0)

    @pl.when(first)
    def _():
        ref[...] = sums

    @pl.when(jnp.logical_not(first))
    def _():
        ref[...] += sums


ROWS = 128


def row_spec(width):
    return pl.BlockSpec((ROWS, width), lambda at, *_: (at, 0))


def first_norm_kernel(moved, order_ref, x_ref, mods_ref, rows_ref, normed_ref):
    rows = load_chunks(x_ref, order_ref, moved)
    rows_ref[...] = rows
    normed, _ = normalize(rows.astype(wide))
    normed_ref[...] = (normed * (1.0 + mods_ref[0, 1:2]) + mods_ref[0, 0:1]).astype(low)


def first_norm(activations, mods, order, deps):
    rows, width = activations.shape
    moved = inside(width, order)
    if not moved:
        activations = take_chunks(activations, order)
    spec = row_spec(width)
    return call(
        partial(first_norm_kernel, moved),
        2.4,
        (rows // ROWS,),
        [spec, whole(mods)],
        [spec, spec],
        [((rows, width), low)] * 2,
        8 * MIB,
        (activations, mods),
        (order,),
        deps,
    )


def cotangent_kernel(moved, order_ref, place_ref, g_ref, mods_ref, rows_ref, branch_ref):
    rows = load_chunks(g_ref, order_ref, moved)
    rows_ref[...] = rows
    branch_ref[...] = (mods_ref[0, 5:6] * rows.astype(wide)).astype(low)


def cotangent_rows(cotangent, mods, order, places, rows, deps):
    width = cotangent.shape[1]
    moved = inside(width, order)
    if not moved:
        cotangent = take_chunks(cotangent, order)
    steps = rows // ROWS
    out_spec = pl.BlockSpec((ROWS, width), lambda part, at, *_: (part * steps + at, 0))
    return call(
        partial(cotangent_kernel, moved),
        2.5,
        (2, steps),
        [
            pl.BlockSpec(
                (ROWS, width), lambda part, at, order, place: (place[part] * steps + at, 0)
            ),
            pl.BlockSpec((1, 6, width), lambda part, at, *_: (part, 0, 0)),
        ],
        [out_spec, out_spec],
        [((2 * rows, width), low)] * 2,
        8 * MIB,
        (cotangent, mods),
        (order, places),
        deps,
    )


def second_norm_kernel(x_ref, mine_ref, sent_ref, mods_ref, middle_ref, branch_ref, normed_ref):
    branch = mine_ref[...] + sent_ref[...].astype(wide)
    branch_ref[...] = branch
    middle = x_ref[...].astype(wide) + mods_ref[0, 2:3] * branch
    middle_ref[...] = middle
    normed, _ = normalize(middle)
    normed_ref[...] = (normed * (1.0 + mods_ref[0, 4:5]) + mods_ref[0, 3:4]).astype(low)


def second_norm(rows_x, mine, sent, mods):
    rows, width = rows_x.shape
    spec = row_spec(width)
    return call(
        second_norm_kernel,
        1.6,
        (rows // ROWS,),
        [spec, spec, spec, whole(mods)],
        [spec, spec, spec],
        [((rows, width), wide)] * 2 + [((rows, width), low)],
        12 * MIB,
        (rows_x, mine, sent, mods),
    )


def finish_kernel(
    moved, order_ref, middle_ref, mine_ref, sent_ref, g_ref, mods_ref, out_ref, sum_ref
):
    branch = mine_ref[...] + sent_ref[...].astype(wide)
    result = (middle_ref[...] + mods_ref[0, 5:6] * branch).astype(low)
    store_chunks(out_ref, order_ref, moved, result)
    add_sums(sum_ref, pl.program_id(0) == 0, [g_ref[...].astype(wide) * branch])


def finish(middle, mine, sent, cot_rows, mods, order, back, deps):
    rows, width = middle.shape
    spec = row_spec(width)
    moved = inside(width, order)
    out, sums = call(
        partial(finish_kernel, moved),
        3.5,
        (rows // ROWS,),
        [spec, spec, spec, spec, whole(mods)],
        [spec, pl.BlockSpec((1, width), lambda *_: (0, 0))],
        [((rows, width), low), ((1, width), wide)],
        12 * MIB,
        (middle, mine, sent, cot_rows, mods),
        (order,),
        deps,
    )
    return (out if moved else take_chunks(out, back)), sums


def second_back_kernel(
    middle_ref, branch_ref, mine_ref, sent_ref, g_ref, mods_ref, grad_ref, gated_ref, sum_ref
):
    upstream = mine_ref[...] + sent_ref[...].astype(wide)
    normed, grad = norm_back(middle_ref[...], upstream, mods_ref[0, 4:5])
    grad = g_ref[...].astype(wide) + grad
    grad_ref[...] = grad
    gated_ref[...] = (mods_ref[0, 2:3] * grad).astype(low)
    add_sums(
        sum_ref,
        pl.program_id(0) == 0,
        [grad * branch_ref[...], upstream, upstream * normed],
    )


def second_back(middle, branch, mine, sent, cot_rows, mods, deps):
    rows, width = middle.shape
    spec = row_spec(width)
    return call(
        second_back_kernel,
        3.2,
        (rows // ROWS,),
        [spec, spec, spec, spec, spec, whole(mods)],
        [spec, spec, pl.BlockSpec((3, width), lambda *_: (0, 0))],
        [((rows, width), wide), ((rows, width), low), ((3, width), wide)],
        16 * MIB,
        (middle, branch, mine, sent, cot_rows, mods),
        deps=deps,
    )


def first_back_kernel(
    moved, order_ref, x_ref, mine_ref, sent_ref, grad_ref, mods_ref, out_ref, sum_ref
):
    upstream = mine_ref[...] + sent_ref[...].astype(wide)
    normed, grad = norm_back(x_ref[...].astype(wide), upstream, mods_ref[0, 1:2])
    store_chunks(out_ref, order_ref, moved, grad_ref[...] + grad)
    add_sums(sum_ref, pl.program_id(0) == 0, [upstream, upstream * normed])


def first_back(rows_x, mine, sent, grad_mid, mods, order, back, deps):
    rows, width = rows_x.shape
    spec = row_spec(width)
    moved = inside(width, order)
    out, sums = call(
        partial(first_back_kernel, moved),
        4.0,
        (rows // ROWS,),
        [spec, spec, spec, spec, whole(mods)],
        [spec, pl.BlockSpec((2, width), lambda *_: (0, 0))],
        [((rows, width), wide), ((2, width), wide)],
        16 * MIB,
        (rows_x, mine, sent, grad_mid, mods),
        (order,),
        deps,
    )
    return (out if moved else take_chunks(out, back)), sums


def piece_list(refs):
    near, far, near_other, far_other, far_x = refs
    return (
        ((near, None), (far, None), (far_x, 0)),
        ((near_other, None), (far_other, None), (far_x, 1)),
    )


def read_piece(piece, start, size):
    ref, place = piece
    if place is None:
        return ref[:, start : start + size]
    return ref[place, :, start : start + size]


TILE = 256
M_ROWS = 320


def part_spec(width, part):
    return pl.BlockSpec((M_ROWS, width), lambda at, *_: (part * (BLOCK // M_ROWS) + at, 0))


def forward_kernel(cols, finish_tile, left_ref, *refs):
    pieces = piece_list(refs[:5])
    tail = refs[5:]
    size = cols[1] - cols[0]
    for side in range(2):
        for start in range(0, size, TILE):
            total = None
            at = 0
            for piece in pieces[side]:
                right = read_piece(piece, cols[0] + start, TILE)
                depth = right.shape[0]
                term = jnp.dot(left_ref[:, at : at + depth], right, preferred_element_type=wide)
                total = term if total is None else total + term
                at += depth
            finish_tile(total, pl.ds(side * size + start, TILE), *tail)


def store_low(total, place, out_ref):
    out_ref[:, place] = total.astype(low)


GELU_A = 0.7978845608028654
GELU_B = 0.044715


def store_gelu(total, place, out_ref, slope_ref):
    square = total * total
    tanh = jnp.tanh(total * (GELU_A + (GELU_A * GELU_B) * square))
    half = 0.5 + 0.5 * tanh
    out_ref[:, place] = (total * half).astype(low)
    inner = GELU_A + (3.0 * GELU_A * GELU_B) * square
    slope_ref[:, place] = (half + 0.5 * total * (1.0 - tanh * tanh) * inner).astype(low)


def store_slope(total, place, slope_ref, out_ref):
    out_ref[:, place] = (total * slope_ref[:, place].astype(wide)).astype(low)


def forward_product(
    left, left_part, pieces, cols, finish_tile, outs, part, bases=(), extra=(), deps=()
):
    depth = left.shape[1]
    size = 2 * (cols[1] - cols[0])
    return call(
        partial(forward_kernel, cols, finish_tile),
        0.8 + size / (300.0 if outs > 1 else 550.0),
        (BLOCK // M_ROWS,),
        [part_spec(depth, left_part)]
        + [whole(piece) for piece in pieces]
        + [part_spec(size, part)] * len(extra),
        [part_spec(size, part)] * outs,
        [((2 * BLOCK, size), low)] * outs,
        24 * MIB,
        (left, *pieces, *extra),
        deps=deps,
        bases=bases,
    )


def backward_kernel(cols, left_ref, *refs):
    pieces = piece_list(refs[:5])
    out_ref = refs[5]
    size = cols[1] - cols[0]
    at = 0
    for own, other in zip(*pieces):
        depth = own[0].shape[-2]
        for start in range(0, depth, TILE):
            total = None
            for side, (ref, place) in enumerate((own, other)):
                index = (pl.ds(start, TILE), pl.ds(cols[0], size))
                right = ref[index] if place is None else ref[(place, *index)]
                term = contract(left_ref[:, side * size : (side + 1) * size], right, 1, 1)
                total = term if total is None else total + term
            out_ref[:, at + start : at + start + TILE] = total.astype(out_ref.dtype)
        at += depth


def backward_product(left, part, pieces, cols, kind, deps=()):
    depth = left.shape[1]
    width = 2 * pieces[0].shape[0]
    return call(
        partial(backward_kernel, cols),
        0.6 + depth / 500.0,
        (BLOCK // M_ROWS,),
        [part_spec(depth, part)] + [whole(piece) for piece in pieces],
        [pl.BlockSpec((M_ROWS, width), lambda at, *_: (at, 0))],
        [((BLOCK, width), kind)],
        24 * MIB,
        (left, *pieces),
        deps=deps,
    )[0]


SLICES = 2


def row_product(lefts, right_ref, start, size):
    total = None
    for part, left_ref in enumerate(lefts):
        term = contract(
            left_ref[:, start : start + size], right_ref[part * BLOCK : (part + 1) * BLOCK], 0, 0
        )
        total = term if total is None else total + term
    return total


def quarter_of(left_ref):
    return left_ref.shape[1] // 4


def sent_kernel(products, *refs):
    step = pl.program_id(0)
    near_ref, far_ref = refs[3 * products :]
    half = pl.num_programs(0) // 2
    at = 0
    for product in range(products):
        *lefts, right_ref = refs[3 * product : 3 * product + 3]
        quarter = quarter_of(lefts[0])
        cols = right_ref.shape[1]
        place = pl.ds(at, cols)
        far_ref[:, place] = row_product(lefts, right_ref, 3 * quarter, quarter).astype(low)

        @pl.when(step >= half)
        def _(lefts=lefts, right_ref=right_ref, place=place, quarter=quarter):
            near_ref[:, place] = row_product(lefts, right_ref, 0, 2 * quarter).astype(low)

        at += cols


def kept_kernel(products, *refs):
    step = pl.program_id(0)
    near_in, far_in, near_keep, far_keep, near_send, far_send = refs[3 * products :]
    half = pl.num_programs(0) // 2
    at = 0
    for product in range(products):
        *lefts, right_ref = refs[3 * product : 3 * product + 3]
        quarter = quarter_of(lefts[0])
        cols = right_ref.shape[1]
        place = pl.ds(at, cols)
        far = row_product(lefts, right_ref, 2 * quarter, quarter) + far_in[:, place].astype(wide)

        @pl.when(step < half)
        def _(lefts=lefts, right_ref=right_ref, place=place, quarter=quarter, far=far):
            near = row_product(lefts, right_ref, 0, 2 * quarter) + near_in[:, place].astype(wide)
            near_keep[:, place] = near[:quarter]
            near_send[:, place] = near[quarter:].astype(low)
            far_keep[:, place] = far

        @pl.when(step >= half)
        def _(place=place, far=far):
            far_send[:, place] = far.astype(low)

        at += cols


def gradient_layout(products):
    width = products[0][0][0].shape[1]
    args, specs, total = [], [], 0
    for *lefts, right in products:
        for array, part in lefts:
            args.append(array)
            specs.append(pl.BlockSpec((BLOCK, width), lambda *_, part=part: (part, 0)))
        cols = right.shape[1] // SLICES
        args.append(right)
        specs.append(pl.BlockSpec((right.shape[0], cols), lambda at, *_: (0, at)))
        total += cols
    return args, specs, SLICES, width // 4, total


def near_spec(rows, cols, steps, late):
    half = steps // 2
    if late:
        return pl.BlockSpec((rows, cols), lambda at, *_: (0, jnp.maximum(at - half, 0)))
    return pl.BlockSpec((rows, cols), lambda at, *_: (0, jnp.minimum(at, half - 1)))


def sent_gradient(products, deps=()):
    args, specs, steps, quarter, cols = gradient_layout(products)
    return call(
        partial(sent_kernel, len(products)),
        3.0,
        (steps,),
        specs,
        [
            near_spec(2 * quarter, cols, steps, True),
            pl.BlockSpec((quarter, cols), lambda at, *_: (0, at)),
        ],
        [((2 * quarter, cols * steps // 2), low), ((quarter, cols * steps), low)],
        24 * MIB,
        args,
        deps=deps,
    )


def kept_gradient(products, moved, deps=()):
    args, specs, steps, quarter, cols = gradient_layout(products)
    size = cols * steps // 2
    early = near_spec(quarter, cols, steps, False)
    near_keep, far_keep, *sent = call(
        partial(kept_kernel, len(products)),
        4.0,
        (steps,),
        specs
        + [
            near_spec(2 * quarter, cols, steps, False),
            pl.BlockSpec((quarter, cols), lambda at, *_: (0, at)),
        ],
        [early, early, early, near_spec(quarter, cols, steps, True)],
        [((quarter, size), wide)] * 2 + [((quarter, size), low)] * 2,
        32 * MIB,
        (*args, *moved),
        deps=deps,
    )
    return (near_keep, far_keep), sent


def third_kernel(near_ref, far_ref, near_in, far_in, keep_ref, send_ref):
    keep_ref[...] = near_ref[...] + near_in[...].astype(wide)
    send_ref[...] = (far_ref[...] + far_in[...].astype(wide)).astype(low)


def third_gradient(kept, moved, deps=()):
    rows, cols = kept[0].shape
    step = min(64, rows)
    spec = pl.BlockSpec((step, cols), lambda at, *_: (at, 0))
    return call(
        third_kernel,
        1.0,
        (rows // step,),
        [spec] * 4,
        [spec] * 2,
        [((rows, cols), wide), ((rows, cols), low)],
        16 * MIB,
        (*kept, *moved),
        deps=deps,
    )


def fourth_kernel(keep_ref, in_ref, out_ref, send_ref):
    half = out_ref.shape[0]
    out_ref[...] = keep_ref[:half] + in_ref[:half].astype(wide)
    send_ref[...] = (keep_ref[half:] + in_ref[half:].astype(wide)).astype(low)


def fourth_gradient(keep, moved, low_axes, deps=()):
    send = None
    for axis, mask in reversed(low_stages(low_axes)[:-1]):
        rows, cols = keep.shape
        keep, send = call(
            fourth_kernel,
            1.0,
            (1,),
            [whole(keep), whole(moved)],
            [pl.BlockSpec((rows // 2, cols), lambda *_: (0, 0))] * 2,
            [((rows // 2, cols), wide), ((rows // 2, cols), low)],
            16 * MIB,
            (keep, moved),
            deps=deps,
        )
        moved = from_xor(send, axis, mask)
    return (keep, moved), send


def lanes_below(shape):
    return lax.broadcasted_iota(jnp.int32, shape, 1) < LANES // 2


def turned(tile):
    return jnp.concatenate([tile[:, LANES // 2 :], tile[:, : LANES // 2]], axis=1)


def head_tiles(x_ref, rows):
    first = x_ref[rows, 0:LANES]
    second = x_ref[rows, LANES : 2 * LANES]
    third = x_ref[rows, 2 * LANES : 3 * LANES]
    return first, second, third


def attend_kernel(kind_ref, x_ref, bias_ref, out_ref, log_ref):
    left = lanes_below((HALF, LANES))
    top = lax.broadcasted_iota(jnp.int32, (LANES, HALF), 0) < LANES // 2
    zero = jnp.zeros((HALF, LANES), low)
    one = jnp.ones((HALF, LANES), low)
    for half in range(2):
        rows = pl.ds(half * HALF, HALF)
        first, second, third = head_tiles(x_ref, rows)
        kind = kind_ref[half]
        sides = (
            (turned(first), jnp.where(left, first * 0.125, zero), jnp.where(left, second, one)),
            (turned(third), jnp.where(left, zero, second * 0.125), jnp.where(left, one, third)),
        )
        parts = []
        for head, (keys, queries, values) in enumerate(sides):
            scores = contract(keys, queries, 1, 1) + bias_ref[head, kind]
            highest = jnp.max(scores, axis=0, keepdims=True)
            weights = jnp.exp(scores - highest).astype(low)
            total = contract(values, weights, 0, 0)
            spot = (1 - head) * (LANES // 2)
            count = total[spot : spot + 1]
            log_ref[0, 2 * half + head : 2 * half + head + 1] = highest + jnp.log(count)
            parts.append(total / count)
        out_ref[rows, :] = jnp.where(top, parts[0], parts[1]).T.astype(low)


def attend_back_kernel(
    kind_ref, x_ref, grad_ref, bias_ref, log_ref, hots_ref, out_ref, table_ref
):
    left = lanes_below((HALF, LANES))
    zero = jnp.zeros((HALF, LANES), low)
    hots = hots_ref[...]
    for half in range(2):
        rows = pl.ds(half * HALF, HALF)
        first, second, third = head_tiles(x_ref, rows)
        grads = grad_ref[rows, :]
        kind = kind_ref[half]
        first_turned, second_turned, third_turned = turned(first), turned(second), turned(third)
        sides = (
            (
                jnp.where(left, first_turned, zero),
                jnp.where(left, first * 0.125, zero),
                second,
                jnp.where(left, grads, zero),
                jnp.where(left, hots, first_turned * 0.125),
            ),
            (
                jnp.where(left, zero, third_turned),
                jnp.where(left, zero, second * 0.125),
                third,
                jnp.where(left, zero, grads),
                jnp.where(left, second_turned * 0.125, hots),
            ),
        )
        query_grad = None
        key_grads = []
        value_grads = []
        for head, (keys, queries, values, grad, queries_turned) in enumerate(sides):
            scores = contract(keys, queries, 1, 1) + bias_ref[head, kind]
            probs = jnp.exp(scores - log_ref[0, 2 * half + head : 2 * half + head + 1])
            grad_probs = contract(values, grad, 1, 1)
            inner = jnp.sum(probs * grad_probs, axis=0, keepdims=True)
            grad_scores = (probs * (grad_probs - inner)).astype(low)
            value_grads.append(jnp.dot(probs.astype(low), grad, preferred_element_type=wide))
            key_grads.append(jnp.dot(grad_scores, queries_turned, preferred_element_type=wide))
            term = contract(keys, grad_scores, 0, 0)
            query_grad = term if query_grad is None else query_grad + term
        table = jnp.where(left, key_grads[0], key_grads[1])
        total = table if half == 0 else total + table
        query_rows = (query_grad * 0.125).T
        out_ref[rows, 0:LANES] = jnp.where(left, query_rows, key_grads[0]).astype(low)
        out_ref[rows, LANES : 2 * LANES] = jnp.where(left, value_grads[0], query_rows).astype(low)
        out_ref[rows, 2 * LANES :] = jnp.where(left, key_grads[1], value_grads[1]).astype(low)
    table_ref[0] = lax.dot_general(
        hots.astype(wide),
        total,
        (((0,), (0,)), ((), ())),
        precision=precise,
        preferred_element_type=wide,
    )


def attention_specs(part):
    return (
        pl.BlockSpec((BLOCK, 3 * LANES), lambda at, *_: (part, at)),
        pl.BlockSpec((BLOCK, LANES), lambda at, *_: (part, at)),
        pl.BlockSpec((2, 2, HALF, HALF), lambda at, *_: (at, 0, 0, 0)),
        pl.BlockSpec((1, 4, HALF), lambda at, *_: (at, 0, 0)),
        pl.BlockSpec((1, LANES, LANES), lambda at, *_: (at, 0, 0)),
    )


def attend(project, part, bias, kinds, bases=(), deps=()):
    pairs = project.shape[1] // (3 * LANES)
    wide_spec, out_spec, bias_spec, log_spec, _ = attention_specs(part)
    return call(
        attend_kernel,
        7.0,
        (pairs,),
        [wide_spec, bias_spec],
        [out_spec, log_spec],
        [((2 * BLOCK, pairs * LANES), low), ((pairs, 4, HALF), wide)],
        24 * MIB,
        (project, bias),
        (kinds,),
        deps,
        bases,
    )


def attend_back(project, grad, part, bias, logs, kinds, bases=(), deps=()):
    pairs = project.shape[1] // (3 * LANES)
    wide_spec, out_spec, bias_spec, log_spec, table_spec = attention_specs(part)
    hots = np.zeros((HALF, LANES), np.float32)
    hots[:, :24] = place_hots()
    hots[:, LANES // 2 : LANES // 2 + 24] = place_hots()
    hots = jnp.asarray(hots, low)
    return call(
        attend_back_kernel,
        11.0,
        (pairs,),
        [wide_spec, out_spec, bias_spec, log_spec, whole(hots)],
        [wide_spec, table_spec],
        [((2 * BLOCK, pairs * 3 * LANES), low), ((pairs, LANES, LANES), wide)],
        24 * MIB,
        (project, grad, bias, logs, hots),
        (kinds,),
        deps,
        bases,
    )


def place_hots():
    places = np.arange(HALF)
    hots = [places // FRAME, places // 8 % 8, places % 8]
    return np.concatenate([np.eye(8, dtype=np.float32)[hot] for hot in hots], axis=1)


def offset_table():
    offsets = np.zeros((45, 24, 24), np.float32)
    for part in range(3):
        for key in range(8):
            for query in range(8):
                offsets[15 * part + query - key + 7, 8 * part + key, 8 * part + query] = 1.0
    return offsets


def terms_kernel(hots_ref, inner_ref, out_ref, done_ref):
    done_ref[...] = jnp.zeros(done_ref.shape, wide)
    terms = jnp.dot(
        hots_ref[...], inner_ref[0], precision=precise, preferred_element_type=wide
    )
    frames = [
        lax.broadcasted_iota(jnp.int32, (HALF, HALF), dim) // FRAME for dim in range(2)
    ]
    out_ref[0, 0] = terms
    out_ref[0, 1] = jnp.where(frames[0] == frames[1], terms, -1e30)


def position_terms(table, deps):
    heads = table.shape[0]
    hots = place_hots()
    spread = np.einsum("oab,ib->oai", offset_table(), hots)
    inner = jnp.einsum("ho,oai->hai", table, spread, precision=precise)
    hots = jnp.asarray(hots)
    return call(
        terms_kernel,
        3.0,
        (heads,),
        [whole(hots), pl.BlockSpec((1, 24, HALF), lambda at, *_: (at, 0, 0))],
        [
            pl.BlockSpec((1, 2, HALF, HALF), lambda at, *_: (at, 0, 0, 0)),
            pl.BlockSpec((8, LANES), lambda *_: (0, 0)),
        ],
        [((heads, 2, HALF, HALF), wide), ((8, LANES), wide)],
        12 * MIB,
        (hots, inner),
        deps=deps,
    )


def table_gradient(sums):
    pairs = sums.shape[0]
    half = LANES // 2
    grads = jnp.stack(
        [sums[:, at : at + 24, at : at + 24] for at in (0, half)], axis=1
    )
    table = jnp.einsum("peab,oab->peo", grads, offset_table(), precision=precise)
    return table.reshape(2 * pairs, 45)


def lane_sums(values):
    rows, cols = values.shape
    values = values * values
    parts = [values[at : at + 8] for at in range(0, rows, 8)]
    total = sum(parts[1:], parts[0])
    parts = [total[:, at : at + LANES] for at in range(0, cols, LANES)]
    total = sum(parts[1:], parts[0])
    return jnp.sum(total, axis=0, keepdims=True)


def lamb_step(first, weight_ref, moment_ref, square_ref, gradient, outs):
    moment_out, square_out, direction_out, sums_out = outs
    weight = weight_ref[...]
    moment, square, direction = lamb_direction(
        weight, moment_ref[...], square_ref[...], gradient
    )
    moment_out[...] = moment
    square_out[...] = square
    direction_out[...] = direction
    sums = jnp.concatenate([lane_sums(weight), lane_sums(direction)], axis=0)

    @pl.when(first)
    def _():
        sums_out[...] = sums

    @pl.when(jnp.logical_not(first))
    def _():
        sums_out[...] += sums


def lamb_kernel(start, weight_ref, moment_ref, square_ref, keep_ref, moved_ref, *outs):
    place = pl.ds(start, weight_ref.shape[1])
    gradient = keep_ref[:, place] + moved_ref[:, place].astype(wide)
    lamb_step(pl.program_id(0) == 0, weight_ref, moment_ref, square_ref, gradient, outs)


def lamb_outs(weight, spec):
    shapes = [(weight.shape, wide)] * 3 + [((2, LANES), wide)]
    return [spec, spec, spec, pl.BlockSpec((2, LANES), lambda *_: (0, 0))], shapes


def lamb(weight, moment, square, terms, start=0, deps=()):
    rows, cols = weight.shape
    step = min(64, rows)
    spec = pl.BlockSpec((step, cols), lambda at, *_: (at, 0))
    term_spec = pl.BlockSpec((step, terms[0].shape[1]), lambda at, *_: (at, 0))
    out_specs, shapes = lamb_outs(weight, spec)
    return call(
        partial(lamb_kernel, start),
        1.5,
        (rows // step,),
        [spec, spec, spec, term_spec, term_spec],
        out_specs,
        shapes,
        16 * MIB,
        (weight, moment, square, *terms),
        deps=deps,
    )


def lamb_ada_kernel(parts, weight_ref, moment_ref, square_ref, *refs):
    gradient = None
    for cond_ref, mod_ref in zip(refs[:parts], refs[parts : 2 * parts]):
        term = contract(cond_ref[...], mod_ref[...], 0, 0)
        gradient = term if gradient is None else gradient + term
    first = pl.program_id(0) == 0
    lamb_step(first, weight_ref, moment_ref, square_ref, gradient, refs[2 * parts :])


def lamb_ada(weight, moment, square, conds, mods, deps):
    rows, cols = weight.shape
    step = 1024
    spec = pl.BlockSpec((rows, step), lambda at, *_: (0, at))
    out_specs, shapes = lamb_outs(weight, spec)
    return call(
        partial(lamb_ada_kernel, len(conds)),
        8.0,
        (cols // step,),
        [spec, spec, spec]
        + [whole(cond) for cond in conds]
        + [pl.BlockSpec((mod.shape[0], step), lambda at, *_: (0, at)) for mod in mods],
        out_specs,
        shapes,
        24 * MIB,
        (weight, moment, square, *conds, *mods),
        deps=deps,
        stream=True,
    )


def update_kernel(terms, copies_ref, *refs):
    total = tree_sum([ref[...] for ref in refs[:terms]])
    norms = jnp.sqrt(jnp.sum(total, axis=1, keepdims=True) * copies_ref[...])
    refs = refs[terms:]
    count = (len(refs) - 1) // 3
    weights, directions, outs = refs[:count], refs[count : 2 * count], refs[2 * count : 3 * count]
    lane = lax.broadcasted_iota(jnp.int32, (1, count), 1)
    stats = [jnp.zeros((1, count), wide)] * 3
    for at in range(count):
        weight_norm, update_norm = norms[2 * at : 2 * at + 1], norms[2 * at + 1 : 2 * at + 2]
        trust = weight_norm / update_norm
        outs[at][...] = weights[at][...] - learn_rate * trust * directions[at][...]
        values = (weight_norm, update_norm, trust)
        stats = [jnp.where(lane == at, value, row) for value, row in zip(values, stats)]
    refs[-1][...] = jnp.concatenate(stats, axis=0)


def update_weights(terms, copies, weights, directions):
    rows = weights[0].shape[0]
    step = min(32, rows)

    def spec(array):
        if array.shape[0] != rows:
            return whole(array)
        return pl.BlockSpec((step, array.shape[1]), lambda at, *_: (at, 0))

    specs = [spec(weight) for weight in weights]
    stats = (3, len(weights))
    return call(
        partial(update_kernel, len(terms)),
        5.0,
        (rows // step,),
        [whole(copies)] + [whole(term) for term in terms] + specs * 2,
        specs + [pl.BlockSpec(stats, lambda *_: (0, 0))],
        [(weight.shape, wide) for weight in weights] + [(stats, wide)],
        24 * MIB,
        (copies, *terms, *weights, *directions),
        stream=True,
    )


def shards(
    low_axes,
    activations,
    cotangent,
    layout,
    band_ids,
    condition,
    qkv_weight,
    qkv_moment,
    qkv_square,
    out_weight,
    out_moment,
    out_square,
    up_weight,
    up_moment,
    up_square,
    down_weight,
    down_moment,
    down_square,
    ada_weight,
    ada_moment,
    ada_square,
    bias_table,
    bias_moment,
    bias_square,
):
    data_axes = (*low_axes, "x")
    model_axes = ("y", "pair")
    model_count = lax.axis_size(model_axes)
    data_count = lax.axis_size(data_axes)
    data_at = lax.axis_index(data_axes)
    model_at = lax.axis_index(model_axes)
    partner_at = model_at + 1 - 2 * lax.axis_index("pair")
    rows_own, width = activations.shape
    heads_own = bias_table.shape[0]
    qkv_cols = qkv_weight.shape[1]
    attn_cols = qkv_cols + out_weight.shape[1]
    hidden_cols = up_weight.shape[1]
    chunk = width // data_count
    bands = condition.shape[0]

    order = chunk_order(low_axes)
    back = jnp.argsort(order).astype(jnp.int32)

    attn_shard = jnp.concatenate([qkv_weight.astype(low), out_weight.astype(low)], axis=1)
    attn_near, attn_far = gather_low(attn_shard, low_axes)
    attn, attn_stack = gather_first(attn_near, attn_far)
    up_halves = gather_low(*gate((up_weight.astype(low),), (attn_far,)), low_axes)
    up_near, up_far = up_halves
    up_halves = gate(up_halves, attn[2:])
    down_halves = gather_low(*gate((down_weight.astype(low),), (up_halves[1],)), low_axes)
    near_both, far, _, far_other, _ = range(5)

    cond_bands = jax.nn.silu(condition).astype(low)
    cond_mine = lax.dynamic_slice_in_dim(cond_bands, data_at * chunk, chunk, 1)
    (cond_mine,) = gate((cond_mine,), (attn_shard,))
    share = ada_weight.shape[1] // model_count
    ada_cols = lax.dynamic_slice_in_dim(ada_weight, model_at * share, share, 1).astype(low)
    mod_bands = jnp.dot(cond_mine, ada_cols, preferred_element_type=wide)
    mod_bands = mod_bands + swap(mod_bands, "x")
    mod_bands, table_own = gate((mod_bands, bias_table), (attn_near,))
    table_two = jnp.concatenate([table_own, swap(table_own, "y")], axis=0)
    halves = jnp.stack(in_pair(mod_bands, "y"), axis=1)
    (halves,) = gate((halves,), (attn_far,))
    halves = jnp.stack(in_pair(halves, "pair"), axis=2)
    for axis, mask in low_stages(low_axes)[:-1]:
        halves = halves + from_xor(halves, axis, mask)
    (halves,) = gate((halves,), (attn[near_both], attn_stack))
    halves = halves + from_xor(halves, *low_stages(low_axes)[-1])
    mod_bands = halves.reshape(condition.shape[0], model_count * share)

    places = jnp.stack([model_at, partner_at]).astype(jnp.int32)
    layouts = jnp.take(layout, places)
    mods = jnp.take(mod_bands, jnp.take(band_ids, places), axis=0)
    mods = jnp.take(mods.reshape(2, 6, data_count, chunk), order, axis=2).reshape(2, 6, width)
    kinds = (jnp.arange(2, dtype=jnp.int32)[None, :] >= 2 - layouts[:, None]).astype(jnp.int32)
    bias, bias_done = position_terms(table_two, (attn[near_both], attn_stack, up_near))

    qkv_range = (0, qkv_cols)
    out_range = (qkv_cols, attn_cols)
    all_range = (0, hidden_cols)

    rows_x, normed_one = first_norm(activations, mods, order, (bias_done, up_far))
    normed_one_other = swap(normed_one, "pair")
    project = forward_product(
        normed_one, 0, attn, qkv_range, store_low, 1, 0, deps=(up_halves[1],)
    )
    (project,) = forward_product(
        normed_one_other, 0, attn, qkv_range, store_low, 1, 1, bases=project
    )
    attended, logs_other = attend(project, 1, bias, kinds[1])
    up = gather_rest(*up_halves, (attended,))
    down_halves = gate(down_halves, up[2:])
    down = gather_rest(*down_halves, (up[near_both],))
    sent = swap(
        backward_product(
            attended, 1, attn, out_range, low, (up[near_both], up[far_other])
        ),
        "pair",
    )
    attended, logs = attend(project, 0, bias, kinds[0], (attended,))
    mine = backward_product(attended, 0, attn, out_range, wide)
    middle, branch_one, normed_two = second_norm(rows_x, mine, sent, mods)
    normed_two_other = swap(normed_two, "pair")
    hidden = forward_product(
        normed_two, 0, up, all_range, store_gelu, 2, 0, deps=(down_halves[1],)
    )
    hidden, slope = forward_product(
        normed_two_other,
        0,
        up,
        all_range,
        store_gelu,
        2,
        1,
        bases=hidden,
        deps=(down[near_both], down[far_other]),
    )


    low_stage = low_stages(low_axes)[-1]
    cot_rows, grad_branch_two = cotangent_rows(cotangent, mods, order, places, rows_own, (bias_done,))
    down_product = (((grad_branch_two, 0), (grad_branch_two, 1), hidden),)
    down_sent = sent_gradient(down_product, (down[near_both], down[far_other]))
    down_sent = gate(down_sent, down[2:])
    down_moved = swap(down_sent[0], "y"), swap(down_sent[1], "x")
    grad_pre = forward_product(
        grad_branch_two,
        1,
        down,
        all_range,
        store_slope,
        1,
        1,
        extra=(slope,),
        deps=(down_sent[0],),
    )
    other_rows = backward_product(grad_pre[0], 1, up, all_range, low)
    sent = swap(other_rows, "pair")
    (grad_pre,) = forward_product(
        grad_branch_two, 0, down, all_range, store_slope, 1, 0, bases=grad_pre, extra=(slope,)
    )
    mine = backward_product(grad_pre, 0, up, all_range, wide)
    sent_two_rows = backward_product(hidden, 1, down, all_range, low, (mine,))
    sent_two = swap(sent_two_rows, "pair")
    down_kept, down_sent = kept_gradient(down_product, down_moved, (sent_two_rows,))
    down_moved = swap(down_sent[0], "x"), swap(down_sent[1], "y")
    grad_mid, grad_branch_one, middle_sums = second_back(
        middle, branch_one, mine, sent, cot_rows, mods, (down_sent[0],)
    )
    grad_branch_one_other = swap(grad_branch_one, "pair")
    up_product = (((normed_two, 0), (normed_two_other, 0), grad_pre),)
    up_sent = sent_gradient(up_product, (grad_branch_one,))
    up_moved = swap(up_sent[0], "y"), swap(up_sent[1], "x")
    grad_attended = forward_product(
        grad_branch_one, 0, attn, out_range, store_low, 1, 0, deps=(up_sent[0],)
    )
    (grad_attended,) = forward_product(
        grad_branch_one_other, 0, attn, out_range, store_low, 1, 1, bases=grad_attended
    )
    grad_project, sums_other = attend_back(
        project, grad_attended, 1, bias, logs_other, kinds[1], deps=(sent_two,)
    )
    other_rows = backward_product(grad_project, 1, attn, qkv_range, low)
    sent = swap(other_rows, "pair")
    down_kept, down_sent = third_gradient(down_kept, down_moved, (other_rows,))
    down_moved = from_xor(down_sent, *low_stage)
    grad_project, sums_own = attend_back(
        project, grad_attended, 0, bias, logs, kinds[0], (grad_project,), (down_sent,)
    )
    qkv_product = (
        ((normed_one, 0), (normed_one_other, 0), grad_project),
        ((grad_branch_one, 0), (grad_branch_one_other, 0), attended),
    )
    qkv_sent = sent_gradient(qkv_product, (sent,))
    qkv_moved = swap(qkv_sent[0], "y"), swap(qkv_sent[1], "x")
    down_terms, down_sent = fourth_gradient(down_kept, down_moved, low_axes, (qkv_sent[0],))
    mine = backward_product(grad_project, 0, attn, qkv_range, wide, (down_sent,))
    up_kept, up_sent = kept_gradient(up_product, up_moved, (mine,))
    up_moved = swap(up_sent[0], "x"), swap(up_sent[1], "y")
    input_grad, input_sums = first_back(
        rows_x, mine, sent, grad_mid, mods, order, back, (up_sent[0],)
    )
    down_update = lamb(down_weight, down_moment, down_square, down_terms, deps=(input_sums,))
    mine_two = backward_product(hidden, 0, down, all_range, wide, (down_update[3],))
    layer_out, gate_two_sum = finish(
        middle, mine_two, sent_two, cot_rows, mods, order, back, ()
    )
    up_kept, up_sent_third = third_gradient(up_kept, up_moved, (gate_two_sum,))
    up_moved = from_xor(up_sent_third, *low_stage)
    up_terms, up_sent = fourth_gradient(up_kept, up_moved, low_axes)
    qkv_kept, qkv_sent = kept_gradient(qkv_product, qkv_moved, (up_sent,))
    qkv_sent_second = qkv_sent[0]
    qkv_moved = swap(qkv_sent[0], "x"), swap(qkv_sent[1], "y")
    qkv_kept, qkv_sent = third_gradient(qkv_kept, qkv_moved)
    qkv_moved = from_xor(qkv_sent, *low_stage)
    qkv_terms, qkv_sent_last = fourth_gradient(qkv_kept, qkv_moved, low_axes)

    grad_mod = jnp.concatenate([input_sums, middle_sums, gate_two_sum], axis=0).astype(low)
    grad_mod = jnp.take(grad_mod.reshape(6, data_count, chunk), back, axis=1)
    band_own = jnp.take(band_ids, model_at).astype(low)
    (sums_own,) = gate((sums_own,), (mine_two,))
    table = table_gradient(sums_own + sums_other).reshape(1, 2 * heads_own * 45)
    table_low = table.astype(low)
    table_rest = (table - table_low.astype(wide)).astype(low)
    message = jnp.concatenate(
        [
            grad_mod.reshape(1, 6 * width),
            jnp.broadcast_to(band_own, (1, LANES)),
            table_low,
            table_rest,
        ],
        axis=1,
    )
    (message,) = gate((message,), (qkv_sent_second,))
    message = in_order(in_order(message, "pair", 0), "y", 0)
    (message,) = gate((message,), (qkv_sent,))
    for axis, mask in low_stages(low_axes)[:-1]:
        message = jnp.concatenate([message, from_xor(message, axis, mask)], axis=0)
    (message,) = gate((message,), (qkv_sent_last,))
    message = jnp.concatenate([message, from_xor(message, *low_stages(low_axes)[-1])], axis=0)
    messages = (message, swap(message, "x"))
    conds, tables = [], []
    y_first = lax.axis_index("y") == 0
    pair_first = lax.axis_index("pair") == 0
    for message in messages:
        band_hot = (
            message[:, 6 * width].astype(jnp.int32)[:, None]
            == jnp.arange(bands, dtype=jnp.int32)[None, :]
        ).astype(low)
        conds.append(jnp.dot(band_hot, cond_mine, preferred_element_type=wide).astype(low))
        shares = message[:, 6 * width + LANES :].astype(wide).reshape(-1, 2, 2, 2, 2, heads_own * 45)
        shares = shares[:, :, :, 0] + shares[:, :, :, 1]
        shares = jnp.where(pair_first, shares[:, :, 0], shares[:, :, 1])
        shares = jnp.where(
            y_first, shares[:, 0, 0] + shares[:, 1, 1], shares[:, 1, 0] + shares[:, 0, 1]
        )
        tables.append(tree_sum(list(shares)))
    table_sum = (tables[0] + tables[1]).reshape(heads_own, 45)

    weights = (qkv_weight, out_weight, up_weight, down_weight, ada_weight, bias_table)
    bias_update = lamb_direction(bias_table, bias_moment, bias_square, table_sum)
    pad = ((0, 4 - heads_own), (0, LANES - 45))
    bias_sums = jnp.stack(
        [
            jnp.sum(jnp.pad(values * values, pad), axis=0)
            for values in (bias_table, bias_update[2])
        ]
    )
    updates = [
        lamb(qkv_weight, qkv_moment, qkv_square, qkv_terms),
        lamb(out_weight, out_moment, out_square, qkv_terms, qkv_cols),
        lamb(up_weight, up_moment, up_square, up_terms, deps=(qkv_sent_last,)),
        down_update,
        lamb_ada(ada_weight, ada_moment, ada_square, conds, messages, (qkv_sent_last,)),
        (*bias_update, bias_sums),
    ]
    copies = np.array([1.0, 1.0, 1.0, 1.0, 1.0 / model_count, 1.0 / data_count], np.float32)
    norm_sums = jnp.concatenate([update[3] for update in updates], axis=0)
    for axis in low_axes:
        norm_sums = sum_over(norm_sums, axis)
    last_axes = ("x", "y", "pair")
    terms = [norm_sums] + [
        from_xor(norm_sums, last_axes, mask) for mask in range(1, lax.axis_size(last_axes))
    ]
    *fresh, lamb_stats = update_weights(
        terms,
        jnp.asarray(np.repeat(copies, 2)[:, None]),
        weights,
        [update[2] for update in updates],
    )
    outputs = [layer_out, input_grad]
    for new, update in zip(fresh, updates):
        outputs += [new, update[0], update[1]]
    return (*outputs, lamb_stats)


def solution(mesh):
    data_count, model_count = mesh.shape["dp"], mesh.shape["mp"]
    low_sizes = cut_sizes(data_count // 2)
    low_axes = tuple(f"low{at}" for at in range(len(low_sizes)))
    view = Mesh(
        mesh.devices.reshape(*low_sizes, 2, model_count // 2, 2), (*low_axes, "x", "y", "pair")
    )
    data = (*low_axes, "x")
    model = ("y", "pair")
    rows = P((*data, *model), None)
    weight = P(data, model)
    ada = P(data, None)
    table = P(model, None)
    return jax.shard_map(
        partial(shards, low_axes),
        mesh=view,
        in_specs=(
            rows,
            P(data, None),
            P(data),
            P(data),
            P(),
            *([weight] * 12),
            *([ada] * 3),
            *([table] * 3),
        ),
        out_specs=(rows, rows, *([weight] * 12), *([ada] * 3), *([table] * 3), P()),
        check_vma=False,
    )
```

```python
from functools import partial

import jax
import jax.numpy as jnp
import numpy as np
from jax import lax
from jax.experimental import pallas as pl
from jax.experimental.pallas import tpu as pltpu
from jax.sharding import Mesh
from jax.sharding import PartitionSpec as P

BLOCK = 640
HALF = BLOCK // 2
FRAME = BLOCK // 10
LANES = 128
STEP = 10

precise = lax.Precision.HIGHEST
beta_first = 0.9
beta_second = 0.999
adam_eps = 1e-06
weight_decay = 0.01
learn_rate = 0.3
norm_eps = 1e-06
low = jnp.bfloat16
wide = jnp.float32
MIB = 1 << 20


def contract(left, right, left_dim, right_dim):
    return lax.dot_general(
        left, right, (((left_dim,), (right_dim,)), ((), ())), preferred_element_type=wide
    )


def lamb_direction(weight, moment, square, gradient):
    moment_new = beta_first * moment + (1.0 - beta_first) * gradient
    square_new = beta_second * square + (1.0 - beta_second) * gradient * gradient
    direction = (
        moment_new
        / (1.0 - beta_first**STEP)
        / (jnp.sqrt(square_new / (1.0 - beta_second**STEP)) + adam_eps)
        + weight_decay * weight
    )
    return (moment_new, square_new, direction)


def cut_sizes(count):
    sizes = []
    while count > 4:
        sizes.append(4)
        count //= 4
    sizes.append(count)
    return sizes


def from_xor(value, axes, mask):
    size = lax.axis_size(axes)
    return lax.ppermute(value, axes, [(at ^ mask, at) for at in range(size)])


def swap(value, axis):
    return from_xor(value, axis, 1)


def tree_sum(terms):
    while len(terms) > 1:
        terms = [terms[at] + terms[at + 1] for at in range(0, len(terms), 2)]
    return terms[0]


def sum_over(value, axes):
    size = lax.axis_size(axes)
    return tree_sum([value] + [from_xor(value, axes, mask) for mask in range(1, size)])


def in_pair(value, axis):
    other = swap(value, axis)
    first = lax.axis_index(axis) == 0
    return jnp.where(first, value, other), jnp.where(first, other, value)


def in_order(value, axis, dim):
    return jnp.concatenate(in_pair(value, axis), axis=dim)


def low_stages(low_axes):
    stages = []
    for axis in low_axes:
        size = lax.axis_size(axis)
        stages += [(axis, 3), (axis, 1)] if size == 4 else [(axis, 1)]
    return stages


def gather_low(shard, low_axes):
    stages = low_stages(low_axes)
    near = shard
    for axis, mask in stages[:-1]:
        near = jnp.concatenate([near, from_xor(near, axis, mask)], axis=0)
    return near, from_xor(near, *stages[-1])


def gather_rest(near, far, after):
    near_x = swap(near, "x")
    (near_x,) = gate((near_x,), after)
    near_both = jnp.concatenate([near, near_x], axis=0)
    far_other = swap(far, "y")
    near_other = swap(near_both, "y")
    far_x = swap(jnp.stack([far, far_other]), "x")
    return (near_both, far, near_other, far_other, far_x)


def gather_first(near, far):
    near_both = jnp.concatenate([near, swap(near, "x")], axis=0)
    (far,) = gate((far,), (near_both,))
    far_other = swap(far, "y")
    (near_both,) = gate((near_both,), (far_other,))
    near_other = swap(near_both, "y")
    stack = jnp.stack([far, far_other])
    return (near_both, far, near_other, far_other, swap(stack, "x")), stack


def chunk_order(low_axes):
    places = [{axis: lax.axis_index(axis) for axis in low_axes}]
    for axis, mask in low_stages(low_axes):
        places = places + [{**place, axis: place[axis] ^ mask} for place in places]
    order = []
    for place in places:
        base = jnp.int32(0)
        for axis in low_axes:
            base = base * lax.axis_size(axis) + place[axis]
        order.append(base)
    half = len(order) // 2
    x_here = lax.axis_index("x")
    full = []
    for part in (order[:half], order[half:]):
        for step in range(2):
            full = full + [base * 2 + (x_here ^ step) for base in part]
    return jnp.stack(full).astype(jnp.int32)


def sum_stages(value, low_axes):
    for axis, mask in low_stages(low_axes):
        value = value + from_xor(value, axis, mask)
    return value + swap(value, "x")


def is_large(shape):
    return np.prod(shape) >= 1 << 15


def stay(array):
    if is_large(array.shape):
        return pltpu.with_memory_space_constraint(array, pltpu.HBM)
    return array


FLOPS_PER_US = 1.15e9


def call(
    kernel,
    cost,
    grid,
    in_specs,
    out_specs,
    out_shapes,
    limit,
    args,
    scalars=(),
    deps=(),
    bases=(),
    stream=False,
):
    taken = len(scalars) + len(args)
    extra = (*bases, *deps)
    if stream:
        args = [stay(array) for array in args]

    def body(*refs):
        kernel(*refs[:taken], *refs[taken + len(extra) :])

    return pl.pallas_call(
        body,
        grid_spec=pltpu.PrefetchScalarGridSpec(
            num_scalar_prefetch=len(scalars),
            grid=grid,
            in_specs=[*in_specs, *[pl.BlockSpec(memory_space=pl.ANY)] * len(extra)],
            out_specs=out_specs,
        ),
        out_shape=[
            pltpu.HBM(shape, dtype)
            if stream and is_large(shape)
            else jax.ShapeDtypeStruct(shape, dtype)
            for shape, dtype in out_shapes
        ],
        input_output_aliases={taken + at: at for at in range(len(bases))},
        cost_estimate=pl.CostEstimate(
            flops=int(cost * FLOPS_PER_US), bytes_accessed=1, transcendentals=0
        ),
        compiler_params=pltpu.CompilerParams(vmem_limit_bytes=limit),
    )(*scalars, *args, *extra)


def gate_kernel(*_):
    pass


def gate(arrays, deps):
    return call(
        gate_kernel,
        0.5,
        (1,),
        [],
        [pl.BlockSpec(memory_space=pl.ANY)] * len(arrays),
        [(array.shape, array.dtype) for array in arrays],
        MIB,
        (),
        deps=deps,
        bases=arrays,
    )


def whole(array):
    zeros = (0,) * array.ndim
    return pl.BlockSpec(array.shape, lambda *_: zeros)


def take_chunks(values, order):
    rows, width = values.shape
    count = order.shape[0]
    return jnp.take(values.reshape(rows, count, width // count), order, axis=1).reshape(rows, width)


def inside(width, order):
    return width // order.shape[0] % LANES == 0


def load_chunks(ref, order_ref, moved):
    if not moved:
        return ref[...]
    count = order_ref.shape[0]
    chunk = ref.shape[1] // count
    return jnp.concatenate(
        [
            ref[:, pl.ds(pl.multiple_of(order_ref[at] * chunk, chunk), chunk)]
            for at in range(count)
        ],
        axis=1,
    )


def store_chunks(ref, order_ref, moved, values):
    if not moved:
        ref[...] = values
        return
    count = order_ref.shape[0]
    chunk = ref.shape[1] // count
    for at in range(count):
        ref[:, pl.ds(pl.multiple_of(order_ref[at] * chunk, chunk), chunk)] = values[
            :, at * chunk : (at + 1) * chunk
        ]


def normalize(values):
    centered = values - jnp.mean(values, axis=-1, keepdims=True)
    inverse = lax.rsqrt(jnp.mean(centered * centered, axis=-1, keepdims=True) + norm_eps)
    return centered * inverse, inverse


def norm_back(values, upstream, scale_row):
    normed, inverse = normalize(values)
    inner = upstream * (1.0 + scale_row)
    grad = (
        inner
        - jnp.mean(inner, axis=-1, keepdims=True)
        - normed * jnp.mean(inner * normed, axis=-1, keepdims=True)
    ) * inverse
    return normed, grad


def add_sums(ref, first, values):
    sums = jnp.concatenate([jnp.sum(value, axis=0, keepdims=True) for value in values], axis=0)

    @pl.when(first)
    def _():
        ref[...] = sums

    @pl.when(jnp.logical_not(first))
    def _():
        ref[...] += sums


ROWS = 128


def row_spec(width):
    return pl.BlockSpec((ROWS, width), lambda at, *_: (at, 0))


def first_norm_kernel(moved, order_ref, x_ref, mods_ref, rows_ref, normed_ref):
    rows = load_chunks(x_ref, order_ref, moved)
    rows_ref[...] = rows
    normed, _ = normalize(rows.astype(wide))
    normed_ref[...] = (normed * (1.0 + mods_ref[0, 1:2]) + mods_ref[0, 0:1]).astype(low)


def first_norm(activations, mods, order, deps):
    rows, width = activations.shape
    moved = inside(width, order)
    if not moved:
        activations = take_chunks(activations, order)
    spec = row_spec(width)
    return call(
        partial(first_norm_kernel, moved),
        2.4,
        (rows // ROWS,),
        [spec, whole(mods)],
        [spec, spec],
        [((rows, width), low)] * 2,
        8 * MIB,
        (activations, mods),
        (order,),
        deps,
    )


def cotangent_kernel(moved, order_ref, place_ref, g_ref, mods_ref, rows_ref, branch_ref):
    rows = load_chunks(g_ref, order_ref, moved)
    rows_ref[...] = rows
    branch_ref[...] = (mods_ref[0, 5:6] * rows.astype(wide)).astype(low)


def cotangent_rows(cotangent, mods, order, places, rows, deps):
    width = cotangent.shape[1]
    moved = inside(width, order)
    if not moved:
        cotangent = take_chunks(cotangent, order)
    steps = rows // ROWS
    out_spec = pl.BlockSpec((ROWS, width), lambda part, at, *_: (part * steps + at, 0))
    return call(
        partial(cotangent_kernel, moved),
        2.5,
        (2, steps),
        [
            pl.BlockSpec(
                (ROWS, width), lambda part, at, order, place: (place[part] * steps + at, 0)
            ),
            pl.BlockSpec((1, 6, width), lambda part, at, *_: (part, 0, 0)),
        ],
        [out_spec, out_spec],
        [((2 * rows, width), low)] * 2,
        8 * MIB,
        (cotangent, mods),
        (order, places),
        deps,
    )


def second_norm_kernel(x_ref, mine_ref, sent_ref, mods_ref, middle_ref, branch_ref, normed_ref):
    branch = mine_ref[...] + sent_ref[...].astype(wide)
    branch_ref[...] = branch
    middle = x_ref[...].astype(wide) + mods_ref[0, 2:3] * branch
    middle_ref[...] = middle
    normed, _ = normalize(middle)
    normed_ref[...] = (normed * (1.0 + mods_ref[0, 4:5]) + mods_ref[0, 3:4]).astype(low)


def second_norm(rows_x, mine, sent, mods):
    rows, width = rows_x.shape
    spec = row_spec(width)
    return call(
        second_norm_kernel,
        1.6,
        (rows // ROWS,),
        [spec, spec, spec, whole(mods)],
        [spec, spec, spec],
        [((rows, width), wide)] * 2 + [((rows, width), low)],
        12 * MIB,
        (rows_x, mine, sent, mods),
    )


def finish_kernel(
    moved, order_ref, middle_ref, mine_ref, sent_ref, g_ref, mods_ref, out_ref, sum_ref
):
    branch = mine_ref[...] + sent_ref[...].astype(wide)
    result = (middle_ref[...] + mods_ref[0, 5:6] * branch).astype(low)
    store_chunks(out_ref, order_ref, moved, result)
    add_sums(sum_ref, pl.program_id(0) == 0, [g_ref[...].astype(wide) * branch])


def finish(middle, mine, sent, cot_rows, mods, order, back, deps):
    rows, width = middle.shape
    spec = row_spec(width)
    moved = inside(width, order)
    out, sums = call(
        partial(finish_kernel, moved),
        3.5,
        (rows // ROWS,),
        [spec, spec, spec, spec, whole(mods)],
        [spec, pl.BlockSpec((1, width), lambda *_: (0, 0))],
        [((rows, width), low), ((1, width), wide)],
        12 * MIB,
        (middle, mine, sent, cot_rows, mods),
        (order,),
        deps,
    )
    return (out if moved else take_chunks(out, back)), sums


def second_back_kernel(
    middle_ref, branch_ref, mine_ref, sent_ref, g_ref, mods_ref, grad_ref, gated_ref, sum_ref
):
    upstream = mine_ref[...] + sent_ref[...].astype(wide)
    normed, grad = norm_back(middle_ref[...], upstream, mods_ref[0, 4:5])
    grad = g_ref[...].astype(wide) + grad
    grad_ref[...] = grad
    gated_ref[...] = (mods_ref[0, 2:3] * grad).astype(low)
    add_sums(
        sum_ref,
        pl.program_id(0) == 0,
        [grad * branch_ref[...], upstream, upstream * normed],
    )


def second_back(middle, branch, mine, sent, cot_rows, mods, deps):
    rows, width = middle.shape
    spec = row_spec(width)
    return call(
        second_back_kernel,
        3.2,
        (rows // ROWS,),
        [spec, spec, spec, spec, spec, whole(mods)],
        [spec, spec, pl.BlockSpec((3, width), lambda *_: (0, 0))],
        [((rows, width), wide), ((rows, width), low), ((3, width), wide)],
        16 * MIB,
        (middle, branch, mine, sent, cot_rows, mods),
        deps=deps,
    )


def first_back_kernel(
    moved, order_ref, x_ref, mine_ref, sent_ref, grad_ref, mods_ref, out_ref, sum_ref
):
    upstream = mine_ref[...] + sent_ref[...].astype(wide)
    normed, grad = norm_back(x_ref[...].astype(wide), upstream, mods_ref[0, 1:2])
    store_chunks(out_ref, order_ref, moved, grad_ref[...] + grad)
    add_sums(sum_ref, pl.program_id(0) == 0, [upstream, upstream * normed])


def first_back(rows_x, mine, sent, grad_mid, mods, order, back, deps):
    rows, width = rows_x.shape
    spec = row_spec(width)
    moved = inside(width, order)
    out, sums = call(
        partial(first_back_kernel, moved),
        4.0,
        (rows // ROWS,),
        [spec, spec, spec, spec, whole(mods)],
        [spec, pl.BlockSpec((2, width), lambda *_: (0, 0))],
        [((rows, width), wide), ((2, width), wide)],
        16 * MIB,
        (rows_x, mine, sent, grad_mid, mods),
        (order,),
        deps,
    )
    return (out if moved else take_chunks(out, back)), sums


def piece_list(refs):
    near, far, near_other, far_other, far_x = refs
    return (
        ((near, None), (far, None), (far_x, 0)),
        ((near_other, None), (far_other, None), (far_x, 1)),
    )


def read_piece(piece, start, size):
    ref, place = piece
    if place is None:
        return ref[:, start : start + size]
    return ref[place, :, start : start + size]


TILE = 256
M_ROWS = 320


def part_spec(width, part):
    return pl.BlockSpec((M_ROWS, width), lambda at, *_: (part * (BLOCK // M_ROWS) + at, 0))


def forward_kernel(cols, finish_tile, left_ref, *refs):
    pieces = piece_list(refs[:5])
    tail = refs[5:]
    size = cols[1] - cols[0]
    for side in range(2):
        for start in range(0, size, TILE):
            total = None
            at = 0
            for piece in pieces[side]:
                right = read_piece(piece, cols[0] + start, TILE)
                depth = right.shape[0]
                term = jnp.dot(left_ref[:, at : at + depth], right, preferred_element_type=wide)
                total = term if total is None else total + term
                at += depth
            finish_tile(total, pl.ds(side * size + start, TILE), *tail)


def store_low(total, place, out_ref):
    out_ref[:, place] = total.astype(low)


GELU_A = 0.7978845608028654
GELU_B = 0.044715


def store_gelu(total, place, out_ref, slope_ref):
    square = total * total
    tanh = jnp.tanh(total * (GELU_A + (GELU_A * GELU_B) * square))
    half = 0.5 + 0.5 * tanh
    out_ref[:, place] = (total * half).astype(low)
    inner = GELU_A + (3.0 * GELU_A * GELU_B) * square
    slope_ref[:, place] = (half + 0.5 * total * (1.0 - tanh * tanh) * inner).astype(low)


def store_slope(total, place, slope_ref, out_ref):
    out_ref[:, place] = (total * slope_ref[:, place].astype(wide)).astype(low)


def forward_product(
    left, left_part, pieces, cols, finish_tile, outs, part, bases=(), extra=(), deps=()
):
    depth = left.shape[1]
    size = 2 * (cols[1] - cols[0])
    return call(
        partial(forward_kernel, cols, finish_tile),
        0.8 + size / (300.0 if outs > 1 else 550.0),
        (BLOCK // M_ROWS,),
        [part_spec(depth, left_part)]
        + [whole(piece) for piece in pieces]
        + [part_spec(size, part)] * len(extra),
        [part_spec(size, part)] * outs,
        [((2 * BLOCK, size), low)] * outs,
        24 * MIB,
        (left, *pieces, *extra),
        deps=deps,
        bases=bases,
    )


def backward_kernel(cols, left_ref, *refs):
    pieces = piece_list(refs[:5])
    out_ref = refs[5]
    size = cols[1] - cols[0]
    at = 0
    for own, other in zip(*pieces):
        depth = own[0].shape[-2]
        for start in range(0, depth, TILE):
            total = None
            for side, (ref, place) in enumerate((own, other)):
                index = (pl.ds(start, TILE), pl.ds(cols[0], size))
                right = ref[index] if place is None else ref[(place, *index)]
                term = contract(left_ref[:, side * size : (side + 1) * size], right, 1, 1)
                total = term if total is None else total + term
            out_ref[:, at + start : at + start + TILE] = total.astype(out_ref.dtype)
        at += depth


def backward_product(left, part, pieces, cols, kind, deps=()):
    depth = left.shape[1]
    width = 2 * pieces[0].shape[0]
    return call(
        partial(backward_kernel, cols),
        0.6 + depth / 500.0,
        (BLOCK // M_ROWS,),
        [part_spec(depth, part)] + [whole(piece) for piece in pieces],
        [pl.BlockSpec((M_ROWS, width), lambda at, *_: (at, 0))],
        [((BLOCK, width), kind)],
        24 * MIB,
        (left, *pieces),
        deps=deps,
    )[0]


SLICES = 2


def row_product(lefts, right_ref, start, size):
    total = None
    for part, left_ref in enumerate(lefts):
        term = contract(
            left_ref[:, start : start + size], right_ref[part * BLOCK : (part + 1) * BLOCK], 0, 0
        )
        total = term if total is None else total + term
    return total


def quarter_of(left_ref):
    return left_ref.shape[1] // 4


def sent_kernel(products, *refs):
    step = pl.program_id(0)
    near_ref, far_ref = refs[3 * products :]
    half = pl.num_programs(0) // 2
    at = 0
    for product in range(products):
        *lefts, right_ref = refs[3 * product : 3 * product + 3]
        quarter = quarter_of(lefts[0])
        cols = right_ref.shape[1]
        place = pl.ds(at, cols)
        far_ref[:, place] = row_product(lefts, right_ref, 3 * quarter, quarter).astype(low)

        @pl.when(step >= half)
        def _(lefts=lefts, right_ref=right_ref, place=place, quarter=quarter):
            near_ref[:, place] = row_product(lefts, right_ref, 0, 2 * quarter).astype(low)

        at += cols


def kept_kernel(products, *refs):
    step = pl.program_id(0)
    near_in, far_in, near_keep, far_keep, near_send, far_send = refs[3 * products :]
    half = pl.num_programs(0) // 2
    at = 0
    for product in range(products):
        *lefts, right_ref = refs[3 * product : 3 * product + 3]
        quarter = quarter_of(lefts[0])
        cols = right_ref.shape[1]
        place = pl.ds(at, cols)
        far = row_product(lefts, right_ref, 2 * quarter, quarter) + far_in[:, place].astype(wide)

        @pl.when(step < half)
        def _(lefts=lefts, right_ref=right_ref, place=place, quarter=quarter, far=far):
            near = row_product(lefts, right_ref, 0, 2 * quarter) + near_in[:, place].astype(wide)
            near_keep[:, place] = near[:quarter]
            near_send[:, place] = near[quarter:].astype(low)
            far_keep[:, place] = far

        @pl.when(step >= half)
        def _(place=place, far=far):
            far_send[:, place] = far.astype(low)

        at += cols


def gradient_layout(products):
    width = products[0][0][0].shape[1]
    args, specs, total = [], [], 0
    for *lefts, right in products:
        for array, part in lefts:
            args.append(array)
            specs.append(pl.BlockSpec((BLOCK, width), lambda *_, part=part: (part, 0)))
        cols = right.shape[1] // SLICES
        args.append(right)
        specs.append(pl.BlockSpec((right.shape[0], cols), lambda at, *_: (0, at)))
        total += cols
    return args, specs, SLICES, width // 4, total


def near_spec(rows, cols, steps, late):
    half = steps // 2
    if late:
        return pl.BlockSpec((rows, cols), lambda at, *_: (0, jnp.maximum(at - half, 0)))
    return pl.BlockSpec((rows, cols), lambda at, *_: (0, jnp.minimum(at, half - 1)))


def sent_gradient(products, deps=()):
    args, specs, steps, quarter, cols = gradient_layout(products)
    return call(
        partial(sent_kernel, len(products)),
        3.0,
        (steps,),
        specs,
        [
            near_spec(2 * quarter, cols, steps, True),
            pl.BlockSpec((quarter, cols), lambda at, *_: (0, at)),
        ],
        [((2 * quarter, cols * steps // 2), low), ((quarter, cols * steps), low)],
        24 * MIB,
        args,
        deps=deps,
    )


def kept_gradient(products, moved, deps=()):
    args, specs, steps, quarter, cols = gradient_layout(products)
    size = cols * steps // 2
    early = near_spec(quarter, cols, steps, False)
    near_keep, far_keep, *sent = call(
        partial(kept_kernel, len(products)),
        4.0,
        (steps,),
        specs
        + [
            near_spec(2 * quarter, cols, steps, False),
            pl.BlockSpec((quarter, cols), lambda at, *_: (0, at)),
        ],
        [early, early, early, near_spec(quarter, cols, steps, True)],
        [((quarter, size), wide)] * 2 + [((quarter, size), low)] * 2,
        32 * MIB,
        (*args, *moved),
        deps=deps,
    )
    return (near_keep, far_keep), sent


def third_kernel(near_ref, far_ref, near_in, far_in, keep_ref, send_ref):
    keep_ref[...] = near_ref[...] + near_in[...].astype(wide)
    send_ref[...] = (far_ref[...] + far_in[...].astype(wide)).astype(low)


def third_gradient(kept, moved, deps=()):
    rows, cols = kept[0].shape
    step = min(64, rows)
    spec = pl.BlockSpec((step, cols), lambda at, *_: (at, 0))
    return call(
        third_kernel,
        1.0,
        (rows // step,),
        [spec] * 4,
        [spec] * 2,
        [((rows, cols), wide), ((rows, cols), low)],
        16 * MIB,
        (*kept, *moved),
        deps=deps,
    )


def fourth_kernel(keep_ref, in_ref, out_ref, send_ref):
    half = out_ref.shape[0]
    out_ref[...] = keep_ref[:half] + in_ref[:half].astype(wide)
    send_ref[...] = (keep_ref[half:] + in_ref[half:].astype(wide)).astype(low)


def fourth_gradient(keep, moved, low_axes, deps=()):
    send = None
    for axis, mask in reversed(low_stages(low_axes)[:-1]):
        rows, cols = keep.shape
        keep, send = call(
            fourth_kernel,
            1.0,
            (1,),
            [whole(keep), whole(moved)],
            [pl.BlockSpec((rows // 2, cols), lambda *_: (0, 0))] * 2,
            [((rows // 2, cols), wide), ((rows // 2, cols), low)],
            16 * MIB,
            (keep, moved),
            deps=deps,
        )
        moved = from_xor(send, axis, mask)
    return (keep, moved), send


def lanes_below(shape):
    return lax.broadcasted_iota(jnp.int32, shape, 1) < LANES // 2


def turned(tile):
    return jnp.concatenate([tile[:, LANES // 2 :], tile[:, : LANES // 2]], axis=1)


def head_tiles(x_ref, rows):
    first = x_ref[rows, 0:LANES]
    second = x_ref[rows, LANES : 2 * LANES]
    third = x_ref[rows, 2 * LANES : 3 * LANES]
    return first, second, third


def attend_kernel(kind_ref, x_ref, bias_ref, out_ref, log_ref):
    left = lanes_below((HALF, LANES))
    top = lax.broadcasted_iota(jnp.int32, (LANES, HALF), 0) < LANES // 2
    zero = jnp.zeros((HALF, LANES), low)
    one = jnp.ones((HALF, LANES), low)
    for half in range(2):
        rows = pl.ds(half * HALF, HALF)
        first, second, third = head_tiles(x_ref, rows)
        kind = kind_ref[half]
        sides = (
            (turned(first), jnp.where(left, first * 0.125, zero), jnp.where(left, second, one)),
            (turned(third), jnp.where(left, zero, second * 0.125), jnp.where(left, one, third)),
        )
        parts = []
        for head, (keys, queries, values) in enumerate(sides):
            scores = contract(keys, queries, 1, 1) + bias_ref[head, kind]
            highest = jnp.max(scores, axis=0, keepdims=True)
            weights = jnp.exp(scores - highest).astype(low)
            total = contract(values, weights, 0, 0)
            spot = (1 - head) * (LANES // 2)
            count = total[spot : spot + 1]
            log_ref[0, 2 * half + head : 2 * half + head + 1] = highest + jnp.log(count)
            parts.append(total / count)
        out_ref[rows, :] = jnp.where(top, parts[0], parts[1]).T.astype(low)


def attend_back_kernel(
    kind_ref, x_ref, grad_ref, bias_ref, log_ref, hots_ref, out_ref, table_ref
):
    left = lanes_below((HALF, LANES))
    zero = jnp.zeros((HALF, LANES), low)
    hots = hots_ref[...]
    for half in range(2):
        rows = pl.ds(half * HALF, HALF)
        first, second, third = head_tiles(x_ref, rows)
        grads = grad_ref[rows, :]
        kind = kind_ref[half]
        first_turned, second_turned, third_turned = turned(first), turned(second), turned(third)
        sides = (
            (
                jnp.where(left, first_turned, zero),
                jnp.where(left, first * 0.125, zero),
                second,
                jnp.where(left, grads, zero),
                jnp.where(left, hots, first_turned * 0.125),
            ),
            (
                jnp.where(left, zero, third_turned),
                jnp.where(left, zero, second * 0.125),
                third,
                jnp.where(left, zero, grads),
                jnp.where(left, second_turned * 0.125, hots),
            ),
        )
        query_grad = None
        key_grads = []
        value_grads = []
        for head, (keys, queries, values, grad, queries_turned) in enumerate(sides):
            scores = contract(keys, queries, 1, 1) + bias_ref[head, kind]
            probs = jnp.exp(scores - log_ref[0, 2 * half + head : 2 * half + head + 1])
            grad_probs = contract(values, grad, 1, 1)
            inner = jnp.sum(probs * grad_probs, axis=0, keepdims=True)
            grad_scores = (probs * (grad_probs - inner)).astype(low)
            value_grads.append(jnp.dot(probs.astype(low), grad, preferred_element_type=wide))
            key_grads.append(jnp.dot(grad_scores, queries_turned, preferred_element_type=wide))
            term = contract(keys, grad_scores, 0, 0)
            query_grad = term if query_grad is None else query_grad + term
        table = jnp.where(left, key_grads[0], key_grads[1])
        total = table if half == 0 else total + table
        query_rows = (query_grad * 0.125).T
        out_ref[rows, 0:LANES] = jnp.where(left, query_rows, key_grads[0]).astype(low)
        out_ref[rows, LANES : 2 * LANES] = jnp.where(left, value_grads[0], query_rows).astype(low)
        out_ref[rows, 2 * LANES :] = jnp.where(left, key_grads[1], value_grads[1]).astype(low)
    table_ref[0] = lax.dot_general(
        hots.astype(wide),
        total,
        (((0,), (0,)), ((), ())),
        precision=precise,
        preferred_element_type=wide,
    )


def attention_specs(part):
    return (
        pl.BlockSpec((BLOCK, 3 * LANES), lambda at, *_: (part, at)),
        pl.BlockSpec((BLOCK, LANES), lambda at, *_: (part, at)),
        pl.BlockSpec((2, 2, HALF, HALF), lambda at, *_: (at, 0, 0, 0)),
        pl.BlockSpec((1, 4, HALF), lambda at, *_: (at, 0, 0)),
        pl.BlockSpec((1, LANES, LANES), lambda at, *_: (at, 0, 0)),
    )


def attend(project, part, bias, kinds, bases=(), deps=()):
    pairs = project.shape[1] // (3 * LANES)
    wide_spec, out_spec, bias_spec, log_spec, _ = attention_specs(part)
    return call(
        attend_kernel,
        7.0,
        (pairs,),
        [wide_spec, bias_spec],
        [out_spec, log_spec],
        [((2 * BLOCK, pairs * LANES), low), ((pairs, 4, HALF), wide)],
        24 * MIB,
        (project, bias),
        (kinds,),
        deps,
        bases,
    )


def attend_back(project, grad, part, bias, logs, kinds, bases=(), deps=()):
    pairs = project.shape[1] // (3 * LANES)
    wide_spec, out_spec, bias_spec, log_spec, table_spec = attention_specs(part)
    hots = np.zeros((HALF, LANES), np.float32)
    hots[:, :24] = place_hots()
    hots[:, LANES // 2 : LANES // 2 + 24] = place_hots()
    hots = jnp.asarray(hots, low)
    return call(
        attend_back_kernel,
        11.0,
        (pairs,),
        [wide_spec, out_spec, bias_spec, log_spec, whole(hots)],
        [wide_spec, table_spec],
        [((2 * BLOCK, pairs * 3 * LANES), low), ((pairs, LANES, LANES), wide)],
        24 * MIB,
        (project, grad, bias, logs, hots),
        (kinds,),
        deps,
        bases,
    )


def place_hots():
    places = np.arange(HALF)
    hots = [places // FRAME, places // 8 % 8, places % 8]
    return np.concatenate([np.eye(8, dtype=np.float32)[hot] for hot in hots], axis=1)


def offset_table():
    offsets = np.zeros((45, 24, 24), np.float32)
    for part in range(3):
        for key in range(8):
            for query in range(8):
                offsets[15 * part + query - key + 7, 8 * part + key, 8 * part + query] = 1.0
    return offsets


def terms_kernel(hots_ref, inner_ref, out_ref, done_ref):
    done_ref[...] = jnp.zeros(done_ref.shape, wide)
    terms = jnp.dot(
        hots_ref[...], inner_ref[0], precision=precise, preferred_element_type=wide
    )
    frames = [
        lax.broadcasted_iota(jnp.int32, (HALF, HALF), dim) // FRAME for dim in range(2)
    ]
    out_ref[0, 0] = terms
    out_ref[0, 1] = jnp.where(frames[0] == frames[1], terms, -1e30)


def position_terms(table, deps):
    heads = table.shape[0]
    hots = place_hots()
    spread = np.einsum("oab,ib->oai", offset_table(), hots)
    inner = jnp.einsum("ho,oai->hai", table, spread, precision=precise)
    hots = jnp.asarray(hots)
    return call(
        terms_kernel,
        3.0,
        (heads,),
        [whole(hots), pl.BlockSpec((1, 24, HALF), lambda at, *_: (at, 0, 0))],
        [
            pl.BlockSpec((1, 2, HALF, HALF), lambda at, *_: (at, 0, 0, 0)),
            pl.BlockSpec((8, LANES), lambda *_: (0, 0)),
        ],
        [((heads, 2, HALF, HALF), wide), ((8, LANES), wide)],
        12 * MIB,
        (hots, inner),
        deps=deps,
    )


def table_gradient(sums):
    pairs = sums.shape[0]
    half = LANES // 2
    grads = jnp.stack(
        [sums[:, at : at + 24, at : at + 24] for at in (0, half)], axis=1
    )
    table = jnp.einsum("peab,oab->peo", grads, offset_table(), precision=precise)
    return table.reshape(2 * pairs, 45)


def lane_sums(values):
    rows, cols = values.shape
    values = values * values
    parts = [values[at : at + 8] for at in range(0, rows, 8)]
    total = sum(parts[1:], parts[0])
    parts = [total[:, at : at + LANES] for at in range(0, cols, LANES)]
    total = sum(parts[1:], parts[0])
    return jnp.sum(total, axis=0, keepdims=True)


def lamb_step(first, weight_ref, moment_ref, square_ref, gradient, outs):
    moment_out, square_out, direction_out, sums_out = outs
    weight = weight_ref[...]
    moment, square, direction = lamb_direction(
        weight, moment_ref[...], square_ref[...], gradient
    )
    moment_out[...] = moment
    square_out[...] = square
    direction_out[...] = direction
    sums = jnp.concatenate([lane_sums(weight), lane_sums(direction)], axis=0)

    @pl.when(first)
    def _():
        sums_out[...] = sums

    @pl.when(jnp.logical_not(first))
    def _():
        sums_out[...] += sums


def lamb_kernel(start, weight_ref, moment_ref, square_ref, keep_ref, moved_ref, *outs):
    place = pl.ds(start, weight_ref.shape[1])
    gradient = keep_ref[:, place] + moved_ref[:, place].astype(wide)
    lamb_step(pl.program_id(0) == 0, weight_ref, moment_ref, square_ref, gradient, outs)


def lamb_outs(weight, spec):
    shapes = [(weight.shape, wide)] * 3 + [((2, LANES), wide)]
    return [spec, spec, spec, pl.BlockSpec((2, LANES), lambda *_: (0, 0))], shapes


def lamb(weight, moment, square, terms, start=0, deps=()):
    rows, cols = weight.shape
    step = min(64, rows)
    spec = pl.BlockSpec((step, cols), lambda at, *_: (at, 0))
    term_spec = pl.BlockSpec((step, terms[0].shape[1]), lambda at, *_: (at, 0))
    out_specs, shapes = lamb_outs(weight, spec)
    return call(
        partial(lamb_kernel, start),
        1.5,
        (rows // step,),
        [spec, spec, spec, term_spec, term_spec],
        out_specs,
        shapes,
        16 * MIB,
        (weight, moment, square, *terms),
        deps=deps,
    )


def lamb_ada_kernel(parts, weight_ref, moment_ref, square_ref, *refs):
    gradient = None
    for cond_ref, mod_ref in zip(refs[:parts], refs[parts : 2 * parts]):
        term = contract(cond_ref[...], mod_ref[...], 0, 0)
        gradient = term if gradient is None else gradient + term
    first = pl.program_id(0) == 0
    lamb_step(first, weight_ref, moment_ref, square_ref, gradient, refs[2 * parts :])


def lamb_ada(weight, moment, square, conds, mods, deps):
    rows, cols = weight.shape
    step = 1024
    spec = pl.BlockSpec((rows, step), lambda at, *_: (0, at))
    out_specs, shapes = lamb_outs(weight, spec)
    return call(
        partial(lamb_ada_kernel, len(conds)),
        8.0,
        (cols // step,),
        [spec, spec, spec]
        + [whole(cond) for cond in conds]
        + [pl.BlockSpec((mod.shape[0], step), lambda at, *_: (0, at)) for mod in mods],
        out_specs,
        shapes,
        24 * MIB,
        (weight, moment, square, *conds, *mods),
        deps=deps,
        stream=True,
    )


def update_kernel(terms, copies_ref, *refs):
    total = tree_sum([ref[...] for ref in refs[:terms]])
    norms = jnp.sqrt(jnp.sum(total, axis=1, keepdims=True) * copies_ref[...])
    refs = refs[terms:]
    count = (len(refs) - 1) // 3
    weights, directions, outs = refs[:count], refs[count : 2 * count], refs[2 * count : 3 * count]
    lane = lax.broadcasted_iota(jnp.int32, (1, count), 1)
    stats = [jnp.zeros((1, count), wide)] * 3
    for at in range(count):
        weight_norm, update_norm = norms[2 * at : 2 * at + 1], norms[2 * at + 1 : 2 * at + 2]
        trust = weight_norm / update_norm
        outs[at][...] = weights[at][...] - learn_rate * trust * directions[at][...]
        values = (weight_norm, update_norm, trust)
        stats = [jnp.where(lane == at, value, row) for value, row in zip(values, stats)]
    refs[-1][...] = jnp.concatenate(stats, axis=0)


def update_weights(terms, copies, weights, directions):
    rows = weights[0].shape[0]
    step = min(32, rows)

    def spec(array):
        if array.shape[0] != rows:
            return whole(array)
        return pl.BlockSpec((step, array.shape[1]), lambda at, *_: (at, 0))

    specs = [spec(weight) for weight in weights]
    stats = (3, len(weights))
    return call(
        partial(update_kernel, len(terms)),
        5.0,
        (rows // step,),
        [whole(copies)] + [whole(term) for term in terms] + specs * 2,
        specs + [pl.BlockSpec(stats, lambda *_: (0, 0))],
        [(weight.shape, wide) for weight in weights] + [(stats, wide)],
        24 * MIB,
        (copies, *terms, *weights, *directions),
        stream=True,
    )


def shards(
    low_axes,
    activations,
    cotangent,
    layout,
    band_ids,
    condition,
    qkv_weight,
    qkv_moment,
    qkv_square,
    out_weight,
    out_moment,
    out_square,
    up_weight,
    up_moment,
    up_square,
    down_weight,
    down_moment,
    down_square,
    ada_weight,
    ada_moment,
    ada_square,
    bias_table,
    bias_moment,
    bias_square,
):
    data_axes = (*low_axes, "x")
    model_axes = ("y", "pair")
    model_count = lax.axis_size(model_axes)
    data_count = lax.axis_size(data_axes)
    data_at = lax.axis_index(data_axes)
    model_at = lax.axis_index(model_axes)
    partner_at = model_at + 1 - 2 * lax.axis_index("pair")
    rows_own, width = activations.shape
    heads_own = bias_table.shape[0]
    qkv_cols = qkv_weight.shape[1]
    attn_cols = qkv_cols + out_weight.shape[1]
    hidden_cols = up_weight.shape[1]
    chunk = width // data_count
    bands = condition.shape[0]

    order = chunk_order(low_axes)
    back = jnp.argsort(order).astype(jnp.int32)

    attn_shard = jnp.concatenate([qkv_weight.astype(low), out_weight.astype(low)], axis=1)
    attn_near, attn_far = gather_low(attn_shard, low_axes)
    attn, attn_stack = gather_first(attn_near, attn_far)
    up_halves = gather_low(*gate((up_weight.astype(low),), (attn_far,)), low_axes)
    up_near, up_far = up_halves
    up_halves = gate(up_halves, attn[2:])
    down_halves = gather_low(*gate((down_weight.astype(low),), (up_halves[1],)), low_axes)
    near_both, far, _, far_other, _ = range(5)

    cond_bands = jax.nn.silu(condition).astype(low)
    cond_mine = lax.dynamic_slice_in_dim(cond_bands, data_at * chunk, chunk, 1)
    (cond_mine,) = gate((cond_mine,), (attn_shard,))
    share = ada_weight.shape[1] // model_count
    ada_cols = lax.dynamic_slice_in_dim(ada_weight, model_at * share, share, 1).astype(low)
    mod_bands = jnp.dot(cond_mine, ada_cols, preferred_element_type=wide)
    mod_bands = mod_bands + swap(mod_bands, "x")
    mod_bands, table_own = gate((mod_bands, bias_table), (attn_near,))
    table_two = jnp.concatenate([table_own, swap(table_own, "y")], axis=0)
    halves = jnp.stack(in_pair(mod_bands, "y"), axis=1)
    (halves,) = gate((halves,), (attn_far,))
    halves = jnp.stack(in_pair(halves, "pair"), axis=2)
    for axis, mask in low_stages(low_axes)[:-1]:
        halves = halves + from_xor(halves, axis, mask)
    (halves,) = gate((halves,), (attn[near_both], attn_stack))
    halves = halves + from_xor(halves, *low_stages(low_axes)[-1])
    mod_bands = halves.reshape(condition.shape[0], model_count * share)

    places = jnp.stack([model_at, partner_at]).astype(jnp.int32)
    layouts = jnp.take(layout, places)
    mods = jnp.take(mod_bands, jnp.take(band_ids, places), axis=0)
    mods = jnp.take(mods.reshape(2, 6, data_count, chunk), order, axis=2).reshape(2, 6, width)
    kinds = (jnp.arange(2, dtype=jnp.int32)[None, :] >= 2 - layouts[:, None]).astype(jnp.int32)
    bias, bias_done = position_terms(table_two, (attn[near_both], attn_stack, up_near))

    qkv_range = (0, qkv_cols)
    out_range = (qkv_cols, attn_cols)
    all_range = (0, hidden_cols)

    rows_x, normed_one = first_norm(activations, mods, order, (bias_done, up_far))
    normed_one_other = swap(normed_one, "pair")
    project = forward_product(
        normed_one, 0, attn, qkv_range, store_low, 1, 0, deps=(up_halves[1],)
    )
    (project,) = forward_product(
        normed_one_other, 0, attn, qkv_range, store_low, 1, 1, bases=project
    )
    attended, logs_other = attend(project, 1, bias, kinds[1])
    up = gather_rest(*up_halves, (attended,))
    down_halves = gate(down_halves, up[2:])
    down = gather_rest(*down_halves, (up[near_both],))
    sent = swap(
        backward_product(
            attended, 1, attn, out_range, low, (up[near_both], up[far_other])
        ),
        "pair",
    )
    attended, logs = attend(project, 0, bias, kinds[0], (attended,))
    mine = backward_product(attended, 0, attn, out_range, wide)
    middle, branch_one, normed_two = second_norm(rows_x, mine, sent, mods)
    normed_two_other = swap(normed_two, "pair")
    hidden = forward_product(
        normed_two, 0, up, all_range, store_gelu, 2, 0, deps=(down_halves[1],)
    )
    hidden, slope = forward_product(
        normed_two_other,
        0,
        up,
        all_range,
        store_gelu,
        2,
        1,
        bases=hidden,
        deps=(down[near_both], down[far_other]),
    )


    low_stage = low_stages(low_axes)[-1]
    cot_rows, grad_branch_two = cotangent_rows(cotangent, mods, order, places, rows_own, (bias_done,))
    down_product = (((grad_branch_two, 0), (grad_branch_two, 1), hidden),)
    down_sent = sent_gradient(down_product, (down[near_both], down[far_other]))
    down_sent = gate(down_sent, down[2:])
    down_moved = swap(down_sent[0], "y"), swap(down_sent[1], "x")
    grad_pre = forward_product(
        grad_branch_two,
        1,
        down,
        all_range,
        store_slope,
        1,
        1,
        extra=(slope,),
        deps=(down_sent[0],),
    )
    other_rows = backward_product(grad_pre[0], 1, up, all_range, low)
    sent = swap(other_rows, "pair")
    (grad_pre,) = forward_product(
        grad_branch_two, 0, down, all_range, store_slope, 1, 0, bases=grad_pre, extra=(slope,)
    )
    mine = backward_product(grad_pre, 0, up, all_range, wide)
    sent_two_rows = backward_product(hidden, 1, down, all_range, low, (mine,))
    sent_two = swap(sent_two_rows, "pair")
    down_kept, down_sent = kept_gradient(down_product, down_moved, (sent_two_rows,))
    down_moved = swap(down_sent[0], "x"), swap(down_sent[1], "y")
    grad_mid, grad_branch_one, middle_sums = second_back(
        middle, branch_one, mine, sent, cot_rows, mods, (down_sent[0],)
    )
    grad_branch_one_other = swap(grad_branch_one, "pair")
    up_product = (((normed_two, 0), (normed_two_other, 0), grad_pre),)
    up_sent = sent_gradient(up_product, (grad_branch_one,))
    up_moved = swap(up_sent[0], "y"), swap(up_sent[1], "x")
    grad_attended = forward_product(
        grad_branch_one, 0, attn, out_range, store_low, 1, 0, deps=(up_sent[0],)
    )
    (grad_attended,) = forward_product(
        grad_branch_one_other, 0, attn, out_range, store_low, 1, 1, bases=grad_attended
    )
    grad_project, sums_other = attend_back(
        project, grad_attended, 1, bias, logs_other, kinds[1], deps=(sent_two,)
    )
    other_rows = backward_product(grad_project, 1, attn, qkv_range, low)
    sent = swap(other_rows, "pair")
    down_kept, down_sent = third_gradient(down_kept, down_moved, (other_rows,))
    down_moved = from_xor(down_sent, *low_stage)
    grad_project, sums_own = attend_back(
        project, grad_attended, 0, bias, logs, kinds[0], (grad_project,), (down_sent,)
    )
    qkv_product = (
        ((normed_one, 0), (normed_one_other, 0), grad_project),
        ((grad_branch_one, 0), (grad_branch_one_other, 0), attended),
    )
    qkv_sent = sent_gradient(qkv_product, (sent,))
    qkv_moved = swap(qkv_sent[0], "y"), swap(qkv_sent[1], "x")
    down_terms, down_sent = fourth_gradient(down_kept, down_moved, low_axes, (qkv_sent[0],))
    mine = backward_product(grad_project, 0, attn, qkv_range, wide, (down_sent,))
    up_kept, up_sent = kept_gradient(up_product, up_moved, (mine,))
    up_moved = swap(up_sent[0], "x"), swap(up_sent[1], "y")
    input_grad, input_sums = first_back(
        rows_x, mine, sent, grad_mid, mods, order, back, (up_sent[0],)
    )
    down_update = lamb(down_weight, down_moment, down_square, down_terms, deps=(input_sums,))
    mine_two = backward_product(hidden, 0, down, all_range, wide, (down_update[3],))
    layer_out, gate_two_sum = finish(
        middle, mine_two, sent_two, cot_rows, mods, order, back, ()
    )
    up_kept, up_sent_third = third_gradient(up_kept, up_moved, (gate_two_sum,))
    up_moved = from_xor(up_sent_third, *low_stage)
    up_terms, up_sent = fourth_gradient(up_kept, up_moved, low_axes)
    qkv_kept, qkv_sent = kept_gradient(qkv_product, qkv_moved, (up_sent,))
    qkv_sent_second = qkv_sent[0]
    qkv_moved = swap(qkv_sent[0], "x"), swap(qkv_sent[1], "y")
    up_update = lamb(up_weight, up_moment, up_square, up_terms, deps=(qkv_sent_second,))
    qkv_kept, qkv_sent = third_gradient(qkv_kept, qkv_moved, (up_update[3],))
    qkv_moved = from_xor(qkv_sent, *low_stage)
    qkv_terms, qkv_sent_last = fourth_gradient(qkv_kept, qkv_moved, low_axes)

    grad_mod = jnp.concatenate([input_sums, middle_sums, gate_two_sum], axis=0).astype(low)
    grad_mod = jnp.take(grad_mod.reshape(6, data_count, chunk), back, axis=1)
    band_own = jnp.take(band_ids, model_at).astype(low)
    (sums_own,) = gate((sums_own,), (mine_two,))
    table = table_gradient(sums_own + sums_other).reshape(1, 2 * heads_own * 45)
    table_low = table.astype(low)
    table_rest = (table - table_low.astype(wide)).astype(low)
    message = jnp.concatenate(
        [
            grad_mod.reshape(1, 6 * width),
            jnp.broadcast_to(band_own, (1, LANES)),
            table_low,
            table_rest,
        ],
        axis=1,
    )
    (message,) = gate((message,), (qkv_sent_second,))
    message = in_order(in_order(message, "pair", 0), "y", 0)
    (message,) = gate((message,), (qkv_sent,))
    for axis, mask in low_stages(low_axes):
        message = jnp.concatenate([message, from_xor(message, axis, mask)], axis=0)
    (message,) = gate((message,), (qkv_sent_last,))
    messages = (message, swap(message, "x"))
    conds, tables = [], []
    y_first = lax.axis_index("y") == 0
    pair_first = lax.axis_index("pair") == 0
    for message in messages:
        band_hot = (
            message[:, 6 * width].astype(jnp.int32)[:, None]
            == jnp.arange(bands, dtype=jnp.int32)[None, :]
        ).astype(low)
        conds.append(jnp.dot(band_hot, cond_mine, preferred_element_type=wide).astype(low))
        shares = message[:, 6 * width + LANES :].astype(wide).reshape(-1, 2, 2, 2, 2, heads_own * 45)
        shares = shares[:, :, :, 0] + shares[:, :, :, 1]
        shares = jnp.where(pair_first, shares[:, :, 0], shares[:, :, 1])
        shares = jnp.where(
            y_first, shares[:, 0, 0] + shares[:, 1, 1], shares[:, 1, 0] + shares[:, 0, 1]
        )
        tables.append(tree_sum(list(shares)))
    table_sum = (tables[0] + tables[1]).reshape(heads_own, 45)

    weights = (qkv_weight, out_weight, up_weight, down_weight, ada_weight, bias_table)
    bias_update = lamb_direction(bias_table, bias_moment, bias_square, table_sum)
    pad = ((0, 4 - heads_own), (0, LANES - 45))
    bias_sums = jnp.stack(
        [
            jnp.sum(jnp.pad(values * values, pad), axis=0)
            for values in (bias_table, bias_update[2])
        ]
    )
    updates = [
        lamb(qkv_weight, qkv_moment, qkv_square, qkv_terms),
        lamb(out_weight, out_moment, out_square, qkv_terms, qkv_cols),
        up_update,
        down_update,
        lamb_ada(ada_weight, ada_moment, ada_square, conds, messages, (qkv_sent_last,)),
        (*bias_update, bias_sums),
    ]
    copies = np.array([1.0, 1.0, 1.0, 1.0, 1.0 / model_count, 1.0 / data_count], np.float32)
    norm_sums = jnp.concatenate([update[3] for update in updates], axis=0)
    for axis in low_axes:
        norm_sums = sum_over(norm_sums, axis)
    last_axes = ("x", "y", "pair")
    terms = [norm_sums] + [
        from_xor(norm_sums, last_axes, mask) for mask in range(1, lax.axis_size(last_axes))
    ]
    *fresh, lamb_stats = update_weights(
        terms,
        jnp.asarray(np.repeat(copies, 2)[:, None]),
        weights,
        [update[2] for update in updates],
    )
    outputs = [layer_out, input_grad]
    for new, update in zip(fresh, updates):
        outputs += [new, update[0], update[1]]
    return (*outputs, lamb_stats)


def solution(mesh):
    data_count, model_count = mesh.shape["dp"], mesh.shape["mp"]
    low_sizes = cut_sizes(data_count // 2)
    low_axes = tuple(f"low{at}" for at in range(len(low_sizes)))
    view = Mesh(
        mesh.devices.reshape(*low_sizes, 2, model_count // 2, 2), (*low_axes, "x", "y", "pair")
    )
    data = (*low_axes, "x")
    model = ("y", "pair")
    rows = P((*data, *model), None)
    weight = P(data, model)
    ada = P(data, None)
    table = P(model, None)
    return jax.shard_map(
        partial(shards, low_axes),
        mesh=view,
        in_specs=(
            rows,
            P(data, None),
            P(data),
            P(data),
            P(),
            *([weight] * 12),
            *([ada] * 3),
            *([table] * 3),
        ),
        out_specs=(rows, rows, *([weight] * 12), *([ada] * 3), *([table] * 3), P()),
        check_vma=False,
    )
```
